128 devices in a mesh: ctx: 128 (over z, y, x, core).
Axes of the slice: x: 4, y: 4, z: 4, core: 2. Of those that a mesh axis runs over, the one named last changes fastest.
Arguments:
- queries: bfloat16 [32768, 4096], P('ctx'), may hold values from -8 to 8
- keys: bfloat16 [32768, 1024], P('ctx'), may hold values from -8 to 8
- values: bfloat16 [32768, 1024], P('ctx'), may hold values from -6 to 6
- cotangent: bfloat16 [32768, 4096], P('ctx'), may hold values from -6 to 6
- selected: int32 [128, 16], P('ctx'), may hold values from -1 to 62, as said below
Outputs:
- attended: bfloat16 [32768, 4096], P('ctx')
- grad_queries: bfloat16 [32768, 4096], P('ctx')
- grad_keys: bfloat16 [32768, 1024], P('ctx')
- grad_values: bfloat16 [32768, 1024], P('ctx')
The draws below stay inside these ranges and needn't reach their ends.
Inputs may be any that keep to these rules, and one draw needn't show every extreme that they name: `selected`: rows d and e are equal when d // 2 == e // 2. A row of query block b = d // 2 holds min(b, 16) live entries, each naming an earlier key block, and -1 elsewhere; its live entries name different blocks; every block b >= 1 names block b - 1, and the last block names block 0.
All inputs are finite; a program needn't handle non-finite values.
Results may differ from the reference program's by a relative error of at most 0.014.
Values may be sent and summed in bfloat16 or wider, within the bound.
No kernel may reach another device: no remote copies, remote signals or barrier semaphores. Data moves between devices by JAX's collectives and lax.ppermute only.
A program may use at most 192 MiB of HBM per device.

```python
import jax
import jax.numpy as jnp
from jax import lax

HD = 128
QH = 32
KVH = 8
BLOCK = 512
PIECES = 2
TOKENS = 32768
N_CTX = 128


def draw_queries(key, part):
    key = jax.random.fold_in(key, 1)
    group = QH // KVH
    rough = jax.random.truncated_normal(key, -5.0, 5.0, (TOKENS, KVH, group, HD), jnp.float32)
    return rough.reshape(TOKENS, QH * HD).astype(jnp.bfloat16)


def draw_keys(key, part):
    key = jax.random.fold_in(key, 2)
    rough = jax.random.truncated_normal(key, -5.0, 5.0, (TOKENS, KVH, HD), jnp.float32)
    return rough.reshape(TOKENS, KVH * HD).astype(jnp.bfloat16)


def draw_selected(key, part):
    key = jax.random.fold_in(key, 11)
    blocks = N_CTX // PIECES
    width = 2 * KVH
    taken = min(width, blocks)
    first, second, third = jax.random.split(key, 3)
    noise = jax.random.randint(first, (blocks, blocks), 0, 65536)
    popular = (jax.random.randint(second, (blocks,), 0, 6) == 0).astype(jnp.int32) * 65536
    row_index = jnp.arange(blocks, dtype=jnp.int32)[:, None]
    column = jnp.arange(blocks, dtype=jnp.int32)[None, :]
    score = noise + popular[None, :] + jnp.where(column == row_index - 1, 262144, 0)
    score = score + jnp.where((row_index == blocks - 1) & (column == 0), 262144, 0)
    combined = score * 1024 + column
    combined = jnp.where(column < row_index, combined, -1 - column)
    best, order = lax.top_k(combined, taken)
    chosen = jnp.where(best >= 0, order, -1).astype(jnp.int32)
    filler = jnp.full((blocks, width - taken), -1, jnp.int32)
    chosen = jnp.concatenate([chosen, filler], axis=1)
    orders = jax.vmap(lambda sub_key: jax.random.permutation(sub_key, width))(jax.random.split(third, blocks))
    arranged = jnp.take_along_axis(chosen, orders, axis=1)
    return jnp.repeat(arranged, PIECES, axis=0).astype(jnp.int32)


def levels(own_key, shape, cuts, smallest, top_value):
    factor_of, own = 1.0, jax.random.fold_in(own_key, 6)
    for dim, blocks in cuts:
        draws = jnp.exp(jax.random.uniform(jax.random.fold_in(own, dim), (blocks,), jnp.float32, smallest / len(cuts), top_value / len(cuts)))
        factor_of = factor_of * jnp.repeat(draws, shape[dim] // blocks).reshape([-1 if axis == dim else 1 for axis in range(len(shape))])
    return factor_of


def normal_values(rng, dims, scale, bound, cuts=(), held_as=jnp.bfloat16):
    gain = levels(rng, dims, cuts, -0.22, 0.18) if cuts else 1.0
    drawn = jax.random.normal(rng, dims, jnp.float32) * scale * gain
    return jnp.minimum(jnp.maximum(drawn, -bound), bound).astype(held_as)


def setup_inputs(seed: int = 0) -> dict:
    streams_of = jax.random.split(jax.random.key(seed), 6)
    queries = draw_queries(jax.random.fold_in(streams_of[5], 71), 0)
    keys = draw_keys(jax.random.fold_in(streams_of[5], 71), 0)
    values = normal_values(streams_of[2], (TOKENS, KVH * HD), 1.0, 6.0, ((0, 128),))
    cotangent = normal_values(streams_of[3], (TOKENS, QH * HD), 1.0, 6.0, ((0, 128),))
    selected = draw_selected(jax.random.fold_in(streams_of[5], 71), 0)
    return {"queries": queries, "keys": keys, "values": values, "cotangent": cotangent, "selected": selected}


def head_pass(query_head, key_rows, value_rows, valid, cot_head, scale):
    score = jnp.einsum("rgd,ld->grl", query_head.astype(jnp.float32), key_rows.astype(jnp.float32)) * scale
    score = jnp.where(valid[None], score, -1e30)
    top = jnp.max(score, axis=2, keepdims=True)
    raised = jnp.exp(score - top)
    weight = raised / jnp.sum(raised, axis=2, keepdims=True)
    weight_b = weight.astype(jnp.bfloat16)
    attended = jnp.einsum("grl,lc->rgc", weight_b.astype(jnp.float32), value_rows.astype(jnp.float32)).astype(jnp.bfloat16)
    dweight = jnp.einsum("rgc,lc->grl", cot_head.astype(jnp.float32), value_rows.astype(jnp.float32))
    delta = jnp.sum(weight * dweight, axis=2, keepdims=True)
    dscore = (weight * (dweight - delta)).astype(jnp.bfloat16)
    grad_query = (jnp.einsum("grl,ld->rgd", dscore.astype(jnp.float32), key_rows.astype(jnp.float32)) * scale).astype(jnp.bfloat16)
    grad_key = jnp.einsum("grl,rgd->ld", dscore.astype(jnp.float32), query_head.astype(jnp.float32)) * scale
    grad_value = jnp.einsum("grl,rgc->lc", weight_b.astype(jnp.float32), cot_head.astype(jnp.float32))
    return attended, grad_query, jnp.concatenate([grad_key, grad_value], axis=1)


def reference(queries, keys, values, cotangent, selected):
    local_rows = TOKENS // N_CTX
    group = QH // KVH
    width = 2 * KVH
    scale = HD ** -0.5
    packed = jnp.concatenate([keys.reshape(TOKENS, KVH, HD), values.reshape(TOKENS, KVH, HD)], axis=2)
    query_dev = queries.reshape(N_CTX, local_rows, KVH, group, HD)
    cot_dev = cotangent.reshape(N_CTX, local_rows, KVH, group, HD)
    head_of = jnp.arange(width, dtype=jnp.int32) // 2

    def one_device(accum, inputs):
        query_here, cot_here, chosen, device = inputs
        block = device // PIECES
        piece = device % PIECES
        own = lax.dynamic_slice_in_dim(packed, block * BLOCK, BLOCK, 0)
        live = chosen >= 0
        safe = jnp.maximum(chosen, 0).astype(jnp.int32)

        def pick(start, head):
            zero = jnp.zeros((), jnp.int32)
            return lax.dynamic_slice(packed, (start * BLOCK, head, zero), (BLOCK, 1, 2 * HD))[:, 0]

        far = jax.vmap(pick)(safe, head_of)
        all_rows = jnp.concatenate([jnp.transpose(own, (1, 0, 2)), far.reshape(KVH, 2 * BLOCK, 2 * HD)], axis=1)
        query_pos = piece * local_rows + jnp.arange(local_rows, dtype=jnp.int32)
        own_valid = jnp.arange(BLOCK, dtype=jnp.int32)[None, :] <= query_pos[:, None]
        far_valid = jnp.repeat(live.reshape(KVH, 2), BLOCK, axis=1)
        valid = jnp.concatenate([jnp.broadcast_to(own_valid[None], (KVH, local_rows, BLOCK)),
                                 jnp.broadcast_to(far_valid[:, None, :], (KVH, local_rows, 2 * BLOCK))], axis=2)
        attended, grad_query, grad_rows = jax.vmap(head_pass, in_axes=(1, 0, 0, 0, 1, None))(
            query_here, all_rows[..., :HD], all_rows[..., HD:], valid, cot_here, scale)
        own_grad = grad_rows[:, :BLOCK]
        mine = (jnp.arange(BLOCK, dtype=jnp.int32) // local_rows == piece)[None, :, None]
        rounded = lax.optimization_barrier(own_grad.astype(jnp.bfloat16)).astype(jnp.float32)
        own_grad = jnp.where(mine, own_grad, rounded)
        current = lax.dynamic_slice_in_dim(accum, block * BLOCK, BLOCK, 0)
        accum = lax.dynamic_update_slice_in_dim(accum, current + jnp.transpose(own_grad, (1, 0, 2)), block * BLOCK, 0)
        far_grad = lax.optimization_barrier(grad_rows[:, BLOCK:].astype(jnp.bfloat16)).astype(jnp.float32)
        far_grad = far_grad.reshape(width, BLOCK, 2 * HD)
        for index in range(width):
            start = (safe[index] * BLOCK, jnp.asarray(index // 2, jnp.int32), jnp.zeros((), jnp.int32))
            current = lax.dynamic_slice(accum, start, (BLOCK, 1, 2 * HD))
            accum = lax.dynamic_update_slice(accum, current + far_grad[index][:, None, :], start)
        attended = jnp.transpose(attended, (1, 0, 2, 3)).reshape(local_rows, QH * HD)
        grad_query = jnp.transpose(grad_query, (1, 0, 2, 3)).reshape(local_rows, QH * HD)
        return accum, (attended, grad_query)

    start_accum = jnp.zeros((TOKENS, KVH, 2 * HD), jnp.float32)
    devices = jnp.arange(N_CTX, dtype=jnp.int32)
    accum, outputs = lax.scan(one_device, start_accum, (query_dev, cot_dev, selected, devices))
    attended = outputs[0].reshape(TOKENS, QH * HD)
    grad_queries = outputs[1].reshape(TOKENS, QH * HD)
    grad_keys = accum[..., :HD].reshape(TOKENS, KVH * HD).astype(jnp.bfloat16)
    grad_values = accum[..., HD:].reshape(TOKENS, KVH * HD).astype(jnp.bfloat16)
    return (attended, grad_queries, grad_keys, grad_values)
```

```python
import math

import jax
import jax.numpy as jnp
from jax import lax
from jax.experimental import pallas as pl
from jax.experimental.pallas import tpu as pltpu
from jax.sharding import PartitionSpec as P

HD = 128
QH = 32
KVH = 8
BLOCK = 512
ROWS = 256
BLOCKS = 64
HALF = KVH // 2
GROUP = QH // KVH
FAR = 2 * BLOCK
SCALE = HD ** -0.5
SCALE_LOG2 = SCALE * math.log2(math.e)
NN = (((1,), (0,)), ((), ()))
NT = (((1,), (1,)), ((), ()))
TN = (((0,), (0,)), ((), ()))
f32 = jnp.float32
bf16 = jnp.bfloat16

PAIR = [(i, i ^ 1) for i in range(2 * BLOCKS)]
SAME_HALF = [list(range(k, 2 * BLOCKS, 2)) for k in (0, 1)]


def dot(a, b, dims):
    return lax.dot_general(a, b, dims, preferred_element_type=f32)


def pick_kernel(table, shares, out):
    step = pl.program_id(0)
    count = out.shape[0]
    for i in range(count):
        row = (step * count + i) * 2 * HALF
        for h in range(HALF):
            first = jnp.maximum(table[row + 2 * h], 0)
            second = jnp.maximum(table[row + 2 * h + 1], 0)
            for kv in range(2):
                tile = kv * HALF + h
                both = jnp.concatenate(
                    [shares[first, tile].astype(f32), shares[second, tile].astype(f32)], axis=0
                )
                out[i, h, kv] = both.astype(bf16)


def pick(table, shares):
    count = 8
    return pl.pallas_call(
        pick_kernel,
        grid_spec=pltpu.PrefetchScalarGridSpec(
            num_scalar_prefetch=1,
            grid=(BLOCKS // count,),
            in_specs=[pl.BlockSpec(shares.shape, lambda i, t: (0, 0, 0, 0))],
            out_specs=pl.BlockSpec((count, HALF, 2, 16, HD), lambda i, t: (i, 0, 0, 0, 0)),
        ),
        out_shape=jax.ShapeDtypeStruct((BLOCKS, HALF, 2, 16, HD), bf16),
        compiler_params=pltpu.CompilerParams(vmem_limit_bytes=32 * 2**20),
        name="pick",
    )(table, shares)


def add_kernel(table, terms, out, total):
    step = pl.program_id(0)
    count = terms.shape[0]

    @pl.when(step == 0)
    def _():
        total[...] = jnp.zeros_like(total)

    for i in range(count):
        row = (step * count + i) * 2 * HALF
        places = []
        sums = []
        for h in range(HALF):
            for e in range(2):
                block = table[row + 2 * h + e]
                slot = jnp.where(block < 0, BLOCKS, block)
                for kv in range(2):
                    places.append((slot, kv * HALF + h))
                    term = terms[i, h, kv].astype(f32)[8 * e : 8 * e + 8]
                    sums.append(total[slot, kv * HALF + h] + term)
        for place, value in zip(places, sums):
            total[place] = value

    @pl.when(step == pl.num_programs(0) - 1)
    def _():
        out[...] = total[:BLOCKS].astype(bf16)


def add_terms(table, terms):
    count = 8
    return pl.pallas_call(
        add_kernel,
        grid_spec=pltpu.PrefetchScalarGridSpec(
            num_scalar_prefetch=1,
            grid=(BLOCKS // count,),
            in_specs=[pl.BlockSpec((count, HALF, 2, 16, HD), lambda i, t: (i, 0, 0, 0, 0))],
            out_specs=pl.BlockSpec((BLOCKS, 2 * HALF, 8, HD), lambda i, t: (0, 0, 0, 0)),
            scratch_shapes=[pltpu.VMEM((BLOCKS + 1, 2 * HALF, 8, HD), f32)],
        ),
        out_shape=jax.ShapeDtypeStruct((BLOCKS, 2 * HALF, 8, HD), bf16),
        compiler_params=pltpu.CompilerParams(vmem_limit_bytes=32 * 2**20),
        name="add_terms",
    )(table, terms)


def attention_kernel(
    chosen, queries, cot, keys, values, far, att, grad_q, grad_k, grad_v, grad_far, K, V, sum_k, sum_v
):
    h = pl.program_id(0)
    g = pl.program_id(1)

    @pl.when(g == 0)
    def _():
        K[:ROWS] = keys[ROWS:]
        K[ROWS:BLOCK] = keys[:ROWS]
        K[BLOCK:] = far[:, 0, 0].reshape(FAR, HD)
        V[:ROWS] = values[ROWS:]
        V[ROWS:BLOCK] = values[:ROWS]
        V[BLOCK:] = far[:, 0, 1].reshape(FAR, HD)
        sum_k[...] = jnp.zeros_like(sum_k)
        sum_v[...] = jnp.zeros_like(sum_v)

    causal = lax.broadcasted_iota(jnp.int32, (ROWS, ROWS), 0) >= lax.broadcasted_iota(
        jnp.int32, (ROWS, ROWS), 1
    )
    first = chosen[2 * h]
    second = chosen[2 * h + 1]

    def run(masked):
        for piece in (0, 1):
            low = ROWS * (1 - piece)
            width = BLOCK + FAR - low
            rows = slice(ROWS * piece, ROWS * piece + ROWS)
            q = queries[rows]
            k = K[low:]
            v = V[low:]
            score = dot(q, k, NT)
            diagonal = jnp.where(causal, score[:, :ROWS], -1e30)
            rest = score[:, ROWS:]
            if masked:
                col = lax.broadcasted_iota(jnp.int32, (1, width - ROWS), 1) - (width - ROWS - FAR)
                entry = jnp.where(jnp.bitwise_and(col, 8) == 0, first, second)
                rest = rest + jnp.where((col >= 0) & (entry < 0), -1e30, 0.0)
            score = jnp.concatenate([diagonal, rest], axis=1)
            top = jnp.max(score, axis=1, keepdims=True)
            raised = jnp.exp2(score * SCALE_LOG2 - top * SCALE_LOG2)
            over = 1.0 / jnp.sum(raised, axis=1, keepdims=True)
            raised_b = raised.astype(bf16)
            out = dot(raised_b, v, NN) * over
            att[rows] = out.astype(bf16)
            cot_over = (cot[rows].astype(f32) * over).astype(bf16)
            delta = jnp.sum(cot_over.astype(f32) * out, axis=1, keepdims=True)
            dweight = dot(cot_over, v, NT)
            dscore = (raised * (dweight - delta)).astype(bf16)
            grad_q[rows] = (dot(dscore, k, NN) * SCALE).astype(bf16)
            sum_v[:, low:] += dot(cot_over, raised_b, TN)
            sum_k[:, low:] += dot(q, dscore, TN)

    alive = jnp.minimum(first, second) >= 0

    @pl.when(alive)
    def _():
        run(False)

    @pl.when(jnp.logical_not(alive))
    def _():
        run(True)

    @pl.when(g == pl.num_programs(1) - 1)
    def _():
        all_k = sum_k[...].T * SCALE
        all_v = sum_v[...].T
        grad_k[:ROWS] = all_k[ROWS:BLOCK]
        grad_k[ROWS:] = all_k[:ROWS]
        grad_v[:ROWS] = all_v[ROWS:BLOCK]
        grad_v[ROWS:] = all_v[:ROWS]
        grad_far[:, 0, 0] = all_k[BLOCK:].astype(bf16).reshape(BLOCKS, 16, HD)
        grad_far[:, 0, 1] = all_v[BLOCK:].astype(bf16).reshape(BLOCKS, 16, HD)


def attention(chosen, queries, cot, keys, values, far):
    per_query = pl.BlockSpec((BLOCK, HD), lambda h, g, c: (0, GROUP * h + g))
    per_key = pl.BlockSpec((BLOCK, HD), lambda h, g, c: (0, h))
    gated = pl.BlockSpec((BLOCKS, 1, 2, 16, HD), lambda h, g, c: (0, h, 0, 0, 0))
    return pl.pallas_call(
        attention_kernel,
        grid_spec=pltpu.PrefetchScalarGridSpec(
            num_scalar_prefetch=1,
            grid=(HALF, GROUP),
            in_specs=[per_query, per_query, per_key, per_key, gated],
            out_specs=[per_query, per_query, per_key, per_key, gated],
            scratch_shapes=[
                pltpu.VMEM((BLOCK + FAR, HD), bf16),
                pltpu.VMEM((BLOCK + FAR, HD), bf16),
                pltpu.VMEM((HD, BLOCK + FAR), f32),
                pltpu.VMEM((HD, BLOCK + FAR), f32),
            ],
        ),
        out_shape=[
            jax.ShapeDtypeStruct(queries.shape, bf16),
            jax.ShapeDtypeStruct(queries.shape, bf16),
            jax.ShapeDtypeStruct(keys.shape, f32),
            jax.ShapeDtypeStruct(keys.shape, f32),
            jax.ShapeDtypeStruct(far.shape, bf16),
        ],
        compiler_params=pltpu.CompilerParams(vmem_limit_bytes=48 * 2**20),
        name="attention",
    )(chosen, queries, cot, keys, values, far)


def spread(x):
    return lax.all_to_all(x, "ctx", 0, 0, axis_index_groups=SAME_HALF, tiled=True)


def halves(x, core):
    width = x.shape[1] // 2
    left, right = x[:, :width], x[:, width:]
    return jnp.where(core == 0, left, right), jnp.where(core == 0, right, left)


def swap(x):
    return lax.ppermute(x, "ctx", PAIR)


def in_order(mine, other, core, axis):
    return jnp.where(
        core == 0,
        jnp.concatenate([mine, other], axis=axis),
        jnp.concatenate([other, mine], axis=axis),
    )


def to_block(x, core):
    mine, other = halves(x, core)
    return in_order(mine, swap(other), core, 0)


def from_block(x, core):
    top, bottom = x[:ROWS], x[ROWS:]
    mine = jnp.where(core == 0, top, bottom)
    other = jnp.where(core == 0, bottom, top)
    return in_order(mine, swap(other), core, 1)


def per_device(queries, keys, values, cotangent, selected):
    core = lax.axis_index("ctx") % 2
    my_keys, other_keys = halves(keys, core)
    my_values, other_values = halves(values, core)
    near = in_order(
        jnp.concatenate([my_keys, my_values], axis=1),
        swap(jnp.concatenate([other_keys, other_values], axis=1)),
        core,
        0,
    )
    shares = jnp.transpose(near.reshape(BLOCKS, 8, 2 * HALF, HD), (0, 2, 1, 3))
    row = jnp.pad(selected.astype(bf16), ((0, 7), (0, HD - selected.shape[1])))
    shares = jnp.concatenate(
        [shares, jnp.broadcast_to(row[None, None], (BLOCKS, 1, 8, HD))], axis=1
    )
    shares = spread(shares)
    table = shares[:, 2 * HALF, 0, : 2 * KVH].astype(jnp.int32)
    table = jnp.where(core == 0, table[:, :KVH], table[:, KVH:]).reshape(-1)
    chosen = jnp.where(core == 0, selected[0, :KVH], selected[0, KVH:])
    far = spread(pick(table, shares))
    block_queries = to_block(queries, core)
    block_cot = to_block(cotangent, core)
    attended, grad_q, grad_k, grad_v, grad_far = attention(
        chosen, block_queries, block_cot, near[:, : HALF * HD], near[:, HALF * HD :], far
    )
    summed = spread(add_terms(table, spread(grad_far)))
    summed = jnp.transpose(summed, (0, 2, 1, 3)).reshape(BLOCK, 2 * HALF * HD).astype(f32)
    grad_k = (grad_k + summed[:, : HALF * HD]).astype(bf16)
    grad_v = (grad_v + summed[:, HALF * HD :]).astype(bf16)
    return (
        from_block(attended, core),
        from_block(grad_q, core),
        from_block(grad_k, core),
        from_block(grad_v, core),
    )


def solution(mesh):
    specs = (P("ctx", None),) * 5
    return jax.shard_map(
        per_device, mesh=mesh, in_specs=specs, out_specs=specs[:4], check_vma=False
    )
```

```python
import math

import jax
import jax.numpy as jnp
from jax import lax
from jax.experimental import pallas as pl
from jax.experimental.pallas import tpu as pltpu
from jax.sharding import PartitionSpec as P

HD = 128
QH = 32
KVH = 8
BLOCK = 512
ROWS = 256
BLOCKS = 64
HALF = KVH // 2
GROUP = QH // KVH
FAR = 2 * BLOCK
SCALE = HD ** -0.5
SCALE_LOG2 = SCALE * math.log2(math.e)
NN = (((1,), (0,)), ((), ()))
NT = (((1,), (1,)), ((), ()))
TN = (((0,), (0,)), ((), ()))
f32 = jnp.float32
bf16 = jnp.bfloat16
LIMIT = 2.0**40

PAIR = [(i, i ^ 1) for i in range(2 * BLOCKS)]
SAME_HALF = [list(range(k, 2 * BLOCKS, 2)) for k in (0, 1)]


def pick_kernel(table, shares, out):
    step = pl.program_id(0)
    count, heads = out.shape[:2]

    def one(i, carry):
        row = (step * count + i) * 2 * heads
        for h in range(heads):
            first = jnp.maximum(table[row + 2 * h], 0)
            second = jnp.maximum(table[row + 2 * h + 1], 0)
            for kv in range(2):
                tile = kv * HALF + h
                both = jnp.concatenate(
                    [shares[first, tile].astype(f32), shares[second, tile].astype(f32)], axis=0
                )
                out[i, h, kv] = both.astype(bf16)
        return carry

    lax.fori_loop(0, count, one, 0, unroll=8)


def pick(table, shares):
    count = 32
    return pl.pallas_call(
        pick_kernel,
        grid_spec=pltpu.PrefetchScalarGridSpec(
            num_scalar_prefetch=1,
            grid=(BLOCKS // count,),
            in_specs=[pl.BlockSpec(shares.shape, lambda i, t: (0, 0, 0, 0))],
            out_specs=pl.BlockSpec((count, HALF, 2, 16, HD), lambda i, t: (i, 0, 0, 0, 0)),
        ),
        out_shape=jax.ShapeDtypeStruct((BLOCKS, HALF, 2, 16, HD), bf16),
        compiler_params=pltpu.CompilerParams(vmem_limit_bytes=60 * 2**20),
        name="pick",
    )(table, shares)


def add_kernel(table, terms, out, total):
    step = pl.program_id(0)
    count, heads = terms.shape[:2]

    @pl.when(step == 0)
    def _():
        total[...] = jnp.zeros_like(total)

    def one(i, carry):
        row = (step * count + i) * 2 * heads
        places = []
        sums = []
        for h in range(heads):
            for e in range(2):
                block = table[row + 2 * h + e]
                slot = jnp.where(block < 0, BLOCKS, block)
                for kv in range(2):
                    place = (slot, kv * heads + h)
                    term = terms[i, h, kv].astype(f32)[8 * e : 8 * e + 8]
                    places.append(place)
                    sums.append(total[place] + term)
        for place, value in zip(places, sums):
            total[place] = value
        return carry

    lax.fori_loop(0, count, one, 0, unroll=8)

    @pl.when(step == pl.num_programs(0) - 1)
    def _():
        out[...] = total[:BLOCKS].astype(bf16)


def add_terms(table, terms):
    count = 16
    tiles = 2 * terms.shape[1]
    whole = lambda i, t: (0, 0, 0, 0)
    return pl.pallas_call(
        add_kernel,
        grid_spec=pltpu.PrefetchScalarGridSpec(
            num_scalar_prefetch=1,
            grid=(BLOCKS // count,),
            in_specs=[pl.BlockSpec((count,) + terms.shape[1:], lambda i, t: (i, 0, 0, 0, 0))],
            out_specs=pl.BlockSpec((BLOCKS, tiles, 8, HD), whole),
            scratch_shapes=[pltpu.VMEM((BLOCKS + 1, tiles, 8, HD), f32)],
        ),
        out_shape=jax.ShapeDtypeStruct((BLOCKS, tiles, 8, HD), bf16),
        compiler_params=pltpu.CompilerParams(vmem_limit_bytes=60 * 2**20),
        name="add_terms",
    )(table, terms)


def finish_kernel(core, mine, other, near_mine, near_other, grad_k, grad_v):
    rows = grad_k.shape[0]
    for side, far, near in ((core[0], mine, near_mine), (1 - core[0], other, near_other)):
        tile = 0
        for out in (grad_k, grad_v):
            for h in range(HALF):
                term = far[:, tile].reshape(rows, HD).astype(f32)
                place = pl.ds(pl.multiple_of((side * HALF + h) * HD, HD), HD)
                out[:, place] = (near[:, HD * tile : HD * tile + HD] + term).astype(bf16)
                tile += 1


def finish(core, mine, other, near):
    steps = 4
    tiles = mine.shape[1]
    chunk = ROWS // 8 // steps
    near_mine, near_other = near
    far = pl.BlockSpec((chunk, tiles, 8, HD), lambda i, c: (i, 0, 0, 0))
    far_mine = pl.BlockSpec((chunk, tiles, 8, HD), lambda i, c: (i + steps * c[0], 0, 0, 0))
    rows = pl.BlockSpec((ROWS // steps, KVH * HD), lambda i, c: (i, 0))
    rows_mine = pl.BlockSpec((ROWS // steps, KVH * HD), lambda i, c: (i + steps * c[0], 0))
    return pl.pallas_call(
        finish_kernel,
        grid_spec=pltpu.PrefetchScalarGridSpec(
            num_scalar_prefetch=1,
            grid=(steps,),
            in_specs=[far_mine, far, rows_mine, rows],
            out_specs=[rows, rows],
        ),
        out_shape=[jax.ShapeDtypeStruct((ROWS, KVH * HD), bf16)] * 2,
        compiler_params=pltpu.CompilerParams(vmem_limit_bytes=12 * 2**20),
        name="finish",
    )(core.reshape(1), mine, other, near_mine, near_other)


def dot(a, b, dims):
    return lax.dot_general(a, b, dims, preferred_element_type=f32)


def cost(heads, keys, products):
    pairs = heads * GROUP * BLOCK * keys
    return pl.CostEstimate(
        flops=products * 4 * pairs * HD, transcendentals=pairs, bytes_accessed=heads * 5 * 2**20
    )


def lanes(values):
    each = HD // len(values)
    lane = lax.broadcasted_iota(jnp.int32, (ROWS, HD), 1)
    out = jnp.broadcast_to(values[-1], (ROWS, HD))
    for i in range(len(values) - 2, -1, -1):
        out = jnp.where(lane < (i + 1) * each, values[i], out)
    return out


def near_scores(q, keys_t, piece):
    score = dot(q, keys_t, NN) * SCALE_LOG2
    shape = (ROWS, ROWS)
    causal = lax.broadcasted_iota(jnp.int32, shape, 0) >= lax.broadcasted_iota(jnp.int32, shape, 1)
    diagonal = jnp.where(causal, score[:, ROWS * piece :], -1e30)
    return jnp.concatenate([score[:, :ROWS], diagonal], axis=1) if piece else diagonal


def near_forward_kernel(queries, keys, values, out, lse, keys_t):
    keys_t[...] = keys[...].T
    for piece in (0, 1):
        rows = slice(ROWS * piece, ROWS * piece + ROWS)
        width = ROWS * piece + ROWS
        found = []
        for g in range(GROUP):
            cols = slice(HD * g, HD * g + HD)
            score = near_scores(queries[rows, cols], keys_t[:, :width], piece)
            top = jnp.max(score, axis=1, keepdims=True)
            raised = jnp.exp2(score - top)
            total = jnp.sum(raised, axis=1, keepdims=True)
            out[rows, cols] = dot(raised.astype(bf16), values[:width], NN) * (1.0 / total)
            found.append(top + jnp.log2(total))
        lse[rows] = lanes(found)


def near_forward(queries, near):
    wide = pl.BlockSpec((BLOCK, GROUP * HD), lambda h: (0, h))
    key = pl.BlockSpec((BLOCK, HD), lambda h: (0, h))
    value = pl.BlockSpec((BLOCK, HD), lambda h: (0, HALF + h))
    return pl.pallas_call(
        near_forward_kernel,
        grid=(HALF,),
        in_specs=[wide, key, value],
        out_specs=[wide, key],
        out_shape=[
            jax.ShapeDtypeStruct(queries.shape, f32),
            jax.ShapeDtypeStruct((BLOCK, HALF * HD), f32),
        ],
        scratch_shapes=[pltpu.VMEM((HD, BLOCK), bf16)],
        compiler_params=pltpu.CompilerParams(vmem_limit_bytes=60 * 2**20),
        cost_estimate=cost(HALF, BLOCK * 3 // 4, 2),
        name="near_forward",
    )(queries, near, near)


def far_kernel(
    chosen, queries, cot, near_out, near_lse, far, att, grad_q, stats, grad_far, keys_t, values_t, sum_k, sum_v
):
    h = pl.program_id(0)
    first = chosen[2 * h]
    second = chosen[2 * h + 1]
    keys_t[...] = far[:, 0, 0].reshape(FAR, HD).T
    values_t[...] = far[:, 0, 1].reshape(FAR, HD).T

    def one(rows, cols, l0, masked, general):
        k = far[:, 0, 0].reshape(FAR, HD)
        v = far[:, 0, 1].reshape(FAR, HD)
        q = queries[rows, cols]
        score = dot(q, keys_t[...], NN) * SCALE_LOG2
        if masked:
            col = lax.broadcasted_iota(jnp.int32, (1, FAR), 1)
            entry = jnp.where(jnp.bitwise_and(col, 8) == 0, first, second)
            score = score + jnp.where(entry < 0, -1e30, 0.0)
        top = jnp.maximum(jnp.max(score, axis=1, keepdims=True), l0) if general else l0
        raised = jnp.exp2(score - top)
        near = jnp.exp2(l0 - top) if general else 1.0
        total = jnp.sum(raised, axis=1, keepdims=True) + near
        over = 1.0 / total
        raised_b = raised.astype(bf16)
        out = (dot(raised_b, v, NN) + near * near_out[rows, cols]) * over
        att[rows, cols] = out.astype(bf16)
        cot_over = (cot[rows, cols].astype(f32) * over).astype(bf16)
        delta = jnp.sum(cot_over.astype(f32) * out, axis=1, keepdims=True)
        dscore = (raised * (dot(cot_over, values_t[...], NN) - delta)).astype(bf16)
        grad_q[rows, cols] = dot(dscore, k, NN)
        sum_v[...] += dot(cot_over, raised_b, TN)
        sum_k[...] += dot(q, dscore, TN)
        return total, top + jnp.log2(total), delta * total

    def run(masked, general):
        sum_k[...] = jnp.zeros_like(sum_k)
        sum_v[...] = jnp.zeros_like(sum_v)

        def half(piece, worst):
            rows = pl.ds(pl.multiple_of(ROWS * piece, ROWS), ROWS)
            found = []
            for g in range(GROUP):
                cols = slice(HD * g, HD * g + HD)
                l0 = near_lse[rows, 32 * g : 32 * g + 1]
                total, lse, delta = one(rows, cols, l0, masked, general)
                worst = jnp.maximum(worst, total)
                found += [lse, delta]
            stats[rows, :] = lanes(found)
            return worst

        return jnp.max(lax.fori_loop(0, 2, half, jnp.zeros((ROWS, 1), f32)))

    worst = run(True, False)

    @pl.when(jnp.logical_not(worst <= LIMIT))
    def _():
        run(True, True)

    grad_far[:, 0, 0] = (sum_k[...].T * SCALE).astype(bf16).reshape(BLOCKS, 16, HD)
    grad_far[:, 0, 1] = sum_v[...].T.astype(bf16).reshape(BLOCKS, 16, HD)


def far_attention(chosen, queries, cot, near_out, near_lse, far):
    heads = far.shape[1]
    wide = pl.BlockSpec((BLOCK, GROUP * HD), lambda h, c: (0, h))
    lse = pl.BlockSpec((BLOCK, HD), lambda h, c: (0, h))
    out_wide = pl.BlockSpec((BLOCK, GROUP * HD), lambda h, c: (0, h))
    out_lse = pl.BlockSpec((BLOCK, HD), lambda h, c: (0, h))
    gated = pl.BlockSpec((BLOCKS, 1, 2, 16, HD), lambda h, c: (0, h, 0, 0, 0))
    return pl.pallas_call(
        far_kernel,
        grid_spec=pltpu.PrefetchScalarGridSpec(
            num_scalar_prefetch=1,
            grid=(heads,),
            in_specs=[wide, wide, wide, lse, gated],
            out_specs=[out_wide, out_wide, out_lse, gated],
            scratch_shapes=[pltpu.VMEM((HD, FAR), bf16)] * 2 + [pltpu.VMEM((HD, FAR), f32)] * 2,
        ),
        out_shape=[
            jax.ShapeDtypeStruct((BLOCK, heads * GROUP * HD), bf16),
            jax.ShapeDtypeStruct((BLOCK, heads * GROUP * HD), f32),
            jax.ShapeDtypeStruct((BLOCK, heads * HD), f32),
            jax.ShapeDtypeStruct(far.shape, bf16),
        ],
        compiler_params=pltpu.CompilerParams(vmem_limit_bytes=60 * 2**20),
        cost_estimate=cost(heads, FAR, 6),
        name="far_attention",
    )(chosen, queries, cot, near_out, near_lse, far)


def near_backward_kernel(queries, cot, keys, values, stats, far_q, grad_q, grad_k, grad_v, keys_t, values_t, sum_k, sum_v):
    keys_t[...] = keys[...].T
    values_t[...] = values[...].T
    sum_k[...] = jnp.zeros_like(sum_k)
    sum_v[...] = jnp.zeros_like(sum_v)
    for piece in (0, 1):
        rows = slice(ROWS * piece, ROWS * piece + ROWS)
        width = ROWS * piece + ROWS
        for g in range(GROUP):
            cols = slice(HD * g, HD * g + HD)
            q = queries[rows, cols]
            c = cot[rows, cols]
            weight = jnp.exp2(near_scores(q, keys_t[:, :width], piece) - stats[rows, 32 * g : 32 * g + 1])
            dweight = dot(c, values_t[:, :width], NN)
            dscore = (weight * (dweight - stats[rows, 32 * g + 16 : 32 * g + 17])).astype(bf16)
            grad_q[rows, cols] = ((far_q[rows, cols] + dot(dscore, keys[:width], NN)) * SCALE).astype(bf16)
            sum_v[:, :width] += dot(c, weight.astype(bf16), TN)
            sum_k[:, :width] += dot(q, dscore, TN)
    grad_k[...] = sum_k[...].T * SCALE
    grad_v[...] = sum_v[...].T


def near_backward(queries, cot, near, stats, far_q):
    heads = stats.shape[1] // HD
    wide = pl.BlockSpec((BLOCK, GROUP * HD), lambda h: (0, h))
    key = pl.BlockSpec((BLOCK, HD), lambda h: (0, h))
    value = pl.BlockSpec((BLOCK, HD), lambda h: (0, HALF + h))
    out_wide = pl.BlockSpec((BLOCK, GROUP * HD), lambda h: (0, h))
    narrow = pl.BlockSpec((BLOCK, HD), lambda h: (0, h))
    return pl.pallas_call(
        near_backward_kernel,
        grid=(heads,),
        in_specs=[wide, wide, key, value, narrow, out_wide],
        out_specs=[out_wide, narrow, narrow],
        out_shape=[jax.ShapeDtypeStruct(far_q.shape, bf16)]
        + [jax.ShapeDtypeStruct((BLOCK, heads * HD), f32)] * 2,
        scratch_shapes=[pltpu.VMEM((HD, BLOCK), bf16)] * 2 + [pltpu.VMEM((HD, BLOCK), f32)] * 2,
        compiler_params=pltpu.CompilerParams(vmem_limit_bytes=60 * 2**20),
        cost_estimate=cost(heads, BLOCK * 3 // 4, 5),
        name="near_backward",
    )(queries, cot, near, near, stats, far_q)


def spread(x):
    return lax.all_to_all(x, "ctx", 0, 0, axis_index_groups=SAME_HALF, tiled=True)


def halves(x, core):
    width = x.shape[1] // 2
    left, right = x[:, :width], x[:, width:]
    return jnp.where(core == 0, left, right), jnp.where(core == 0, right, left)


def swap(x):
    return lax.ppermute(x, "ctx", PAIR)


def in_order(mine, other, core, axis):
    return jnp.where(
        core == 0,
        jnp.concatenate([mine, other], axis=axis),
        jnp.concatenate([other, mine], axis=axis),
    )


def to_block(x, core):
    mine, other = halves(x, core)
    return in_order(mine, swap(other), core, 0)


def others_rows(x, core):
    half = x.shape[0] // 2
    return lax.dynamic_slice_in_dim(x, (1 - core) * half, half, 0)


def my_rows(x, core):
    half = x.shape[0] // 2
    return lax.dynamic_slice_in_dim(x, core * half, half, 0)


def per_device(queries, keys, values, cotangent, selected):
    core = lax.axis_index("ctx") % 2
    my_keys, other_keys = halves(keys, core)
    my_values, other_values = halves(values, core)
    near = in_order(
        jnp.concatenate([my_keys, my_values], axis=1),
        swap(jnp.concatenate([other_keys, other_values], axis=1)),
        core,
        0,
    )
    tiles = jnp.transpose(near.reshape(BLOCKS, 8, 2 * HALF, HD), (0, 2, 1, 3))
    row = jnp.pad(selected.astype(bf16), ((0, 7), (0, HD - selected.shape[1])))
    row = jnp.broadcast_to(row[None, None], (BLOCKS, 1, 8, HD))
    tiles = jnp.concatenate([tiles, row], axis=1)
    shares = spread(tiles)
    block_queries = to_block(queries, core)
    block_cot = to_block(cotangent, core)
    near_out, near_lse = near_forward(block_queries, near)
    shares, near_out, near_lse, block_cot = lax.optimization_barrier(
        (shares, near_out, near_lse, block_cot)
    )
    shares, queries, cotangent = lax.optimization_barrier((shares, queries, cotangent))
    table = shares[:, -1, 0, : 2 * KVH].astype(jnp.int32)
    table = jnp.where(core == 0, table[:, :KVH], table[:, KVH:]).reshape(-1)
    chosen = jnp.where(core == 0, selected[0, :KVH], selected[0, KVH:])
    far = spread(pick(table, shares))
    block_queries = to_block(queries, core)
    block_cot = to_block(cotangent, core)
    near_out, near_lse = near_forward(block_queries, near)
    far, near_out, near_lse, block_cot = lax.optimization_barrier(
        (far, near_out, near_lse, block_cot)
    )
    attended, far_q, stats, grad_far = far_attention(
        chosen, block_queries, block_cot, near_out, near_lse, far
    )
    back = spread(grad_far)
    grad_q, grad_k, grad_v = near_backward(block_queries, block_cot, near, stats, far_q)
    attended, grad_q = lax.optimization_barrier((attended, grad_q))
    near_grad = jnp.concatenate([grad_k, grad_v], axis=1)
    near_other = swap(others_rows(near_grad, core))
    other_attended = swap(others_rows(attended, core))
    other_q = swap(others_rows(grad_q, core))
    back, near_grad, near_other, attended, grad_q, other_attended, other_q = lax.optimization_barrier(
        (back, near_grad, near_other, attended, grad_q, other_attended, other_q)
    )
    summed = spread(add_terms(table, back))
    attended = in_order(my_rows(attended, core), other_attended, core, 1)
    grad_q = in_order(my_rows(grad_q, core), other_q, core, 1)
    summed, attended, grad_q = lax.optimization_barrier((summed, attended, grad_q))
    other = swap(others_rows(summed, core))
    grad_k, grad_v = finish(core, summed, other, (near_grad, near_other))
    return attended, grad_q, grad_k, grad_v


def solution(mesh):
    specs = (P("ctx", None),) * 5
    return jax.shard_map(
        per_device, mesh=mesh, in_specs=specs, out_specs=specs[:4], check_vma=False
    )
```

```python
import math

import jax
import jax.numpy as jnp
from jax import lax
from jax.experimental import pallas as pl
from jax.experimental.pallas import tpu as pltpu
from jax.sharding import PartitionSpec as P

HD = 128
QH = 32
KVH = 8
BLOCK = 512
ROWS = 256
BLOCKS = 64
HALF = KVH // 2
GROUP = QH // KVH
FAR = 2 * BLOCK
SCALE = HD ** -0.5
SCALE_LOG2 = SCALE * math.log2(math.e)
NN = (((1,), (0,)), ((), ()))
NT = (((1,), (1,)), ((), ()))
TN = (((0,), (0,)), ((), ()))
f32 = jnp.float32
bf16 = jnp.bfloat16
LIMIT = 2.0**40

PAIR = [(i, i ^ 1) for i in range(2 * BLOCKS)]
SAME_HALF = [list(range(k, 2 * BLOCKS, 2)) for k in (0, 1)]


def pick_kernel(table, shares, out):
    step = pl.program_id(0)
    count, heads = out.shape[:2]

    def one(i, carry):
        row = (step * count + i) * 2 * heads
        for h in range(heads):
            first = jnp.maximum(table[row + 2 * h], 0)
            second = jnp.maximum(table[row + 2 * h + 1], 0)
            for kv in range(2):
                tile = kv * HALF + h
                out[i, h, kv, :8] = shares[first, tile]
                out[i, h, kv, 8:] = shares[second, tile]
        return carry

    lax.fori_loop(0, count, one, 0, unroll=8)


def pick(table, shares):
    count = 32
    return pl.pallas_call(
        pick_kernel,
        grid_spec=pltpu.PrefetchScalarGridSpec(
            num_scalar_prefetch=1,
            grid=(BLOCKS // count,),
            in_specs=[pl.BlockSpec(shares.shape, lambda i, t: (0, 0, 0, 0))],
            out_specs=pl.BlockSpec((count, HALF, 2, 16, HD), lambda i, t: (i, 0, 0, 0, 0)),
        ),
        out_shape=jax.ShapeDtypeStruct((BLOCKS, HALF, 2, 16, HD), bf16),
        compiler_params=pltpu.CompilerParams(vmem_limit_bytes=16 * 2**20),
        name="pick",
    )(table, shares)


def add_kernel(table, terms, out, total):
    step = pl.program_id(0)
    count, heads = terms.shape[:2]

    @pl.when(step == 0)
    def _():
        total[...] = jnp.zeros_like(total)

    def one(i, carry):
        row = (step * count + i) * 2 * heads
        places = []
        sums = []
        for h in range(heads):
            for e in range(2):
                block = table[row + 2 * h + e]
                slot = jnp.where(block < 0, BLOCKS, block)
                for kv in range(2):
                    place = (slot, kv * heads + h)
                    term = terms[i, h, kv].astype(f32)[8 * e : 8 * e + 8]
                    places.append(place)
                    sums.append(total[place] + term)
        for place, value in zip(places, sums):
            total[place] = value
        return carry

    lax.fori_loop(0, count, one, 0, unroll=8)

    @pl.when(step == pl.num_programs(0) - 1)
    def _():
        out[...] = total[:BLOCKS].astype(bf16)


def add_terms(table, terms):
    count = 16
    tiles = 2 * terms.shape[1]
    whole = lambda i, t: (0, 0, 0, 0)
    return pl.pallas_call(
        add_kernel,
        grid_spec=pltpu.PrefetchScalarGridSpec(
            num_scalar_prefetch=1,
            grid=(BLOCKS // count,),
            in_specs=[pl.BlockSpec((count,) + terms.shape[1:], lambda i, t: (i, 0, 0, 0, 0))],
            out_specs=pl.BlockSpec((BLOCKS, tiles, 8, HD), whole),
            scratch_shapes=[pltpu.VMEM((BLOCKS + 1, tiles, 8, HD), f32)],
        ),
        out_shape=jax.ShapeDtypeStruct((BLOCKS, tiles, 8, HD), bf16),
        compiler_params=pltpu.CompilerParams(vmem_limit_bytes=16 * 2**20),
        name="add_terms",
    )(table, terms)


def finish_kernel(core, mine, other, near_k, near_v, near_other, grad_k, grad_v):
    rows = grad_k.shape[0]
    for side, far in ((core[0], mine), (1 - core[0], other)):
        for kv, (out, near) in enumerate(((grad_k, near_k), (grad_v, near_v))):
            for h in range(HALF):
                tile = kv * HALF + h
                term = far[:, tile].reshape(rows, HD).astype(f32)
                if far is mine:
                    term += near[:, HD * h : HD * h + HD]
                else:
                    term += near_other[:, HD * tile : HD * tile + HD].astype(f32)
                place = pl.ds(pl.multiple_of((side * HALF + h) * HD, HD), HD)
                out[:, place] = term.astype(bf16)


def finish(core, mine, other, near_k, near_v, near_other):
    steps = 4
    tiles = mine.shape[1]
    chunk = ROWS // 8 // steps
    far = pl.BlockSpec((chunk, tiles, 8, HD), lambda i, c: (i, 0, 0, 0))
    far_mine = pl.BlockSpec((chunk, tiles, 8, HD), lambda i, c: (i + steps * c[0], 0, 0, 0))
    rows = pl.BlockSpec((ROWS // steps, KVH * HD), lambda i, c: (i, 0))
    rows_mine = pl.BlockSpec((ROWS // steps, HALF * HD), lambda i, c: (i + steps * c[0], 0))
    return pl.pallas_call(
        finish_kernel,
        grid_spec=pltpu.PrefetchScalarGridSpec(
            num_scalar_prefetch=1,
            grid=(steps,),
            in_specs=[far_mine, far, rows_mine, rows_mine, rows],
            out_specs=[rows, rows],
        ),
        out_shape=[jax.ShapeDtypeStruct((ROWS, KVH * HD), bf16)] * 2,
        compiler_params=pltpu.CompilerParams(vmem_limit_bytes=12 * 2**20),
        name="finish",
    )(core.reshape(1), mine, other, near_k, near_v, near_other)


def dot(a, b, dims):
    return lax.dot_general(a, b, dims, preferred_element_type=f32)


def cost(heads, keys, products):
    pairs = heads * GROUP * BLOCK * keys
    return pl.CostEstimate(
        flops=products * 4 * pairs * HD, transcendentals=pairs, bytes_accessed=heads * 5 * 2**20
    )


def lanes(values):
    each = HD // len(values)
    lane = lax.broadcasted_iota(jnp.int32, (ROWS, HD), 1)
    out = jnp.broadcast_to(values[-1], (ROWS, HD))
    for i in range(len(values) - 2, -1, -1):
        out = jnp.where(lane < (i + 1) * each, values[i], out)
    return out


def near_scores(q, keys_t, piece):
    score = dot(q, keys_t, NN) * SCALE_LOG2
    shape = (ROWS, ROWS)
    causal = lax.broadcasted_iota(jnp.int32, shape, 0) >= lax.broadcasted_iota(jnp.int32, shape, 1)
    diagonal = jnp.where(causal, score[:, ROWS * piece :], -1e30)
    return jnp.concatenate([score[:, :ROWS], diagonal], axis=1) if piece else diagonal


def near_forward_kernel(queries, cot, keys, values, out_t, lse_t, cot_t, keys_t):
    keys_t[...] = keys[...].T
    cot_t[...] = cot[...].T
    for piece in (0, 1):
        rows = slice(ROWS * piece, ROWS * piece + ROWS)
        width = ROWS * piece + ROWS
        found = []
        for g in range(GROUP):
            cols = slice(HD * g, HD * g + HD)
            score = near_scores(queries[rows, cols], keys_t[:, :width], piece)
            top = jnp.max(score, axis=1, keepdims=True)
            raised = jnp.exp2(score - top)
            total = jnp.sum(raised, axis=1, keepdims=True)
            out = dot(raised.astype(bf16), values[:width], NN) * (1.0 / total)
            out_t[cols, rows] = out.T
            found.append(top + jnp.log2(total))
        lse = lanes(found).T
        for g in range(GROUP):
            lse_t[g : g + 1, rows] = lse[HD // GROUP * g : HD // GROUP * g + 1]


def near_forward(queries, cot, near):
    wide = pl.BlockSpec((BLOCK, GROUP * HD), lambda h: (0, h))
    key = pl.BlockSpec((BLOCK, HD), lambda h: (0, h))
    value = pl.BlockSpec((BLOCK, HD), lambda h: (0, HALF + h))
    tall = pl.BlockSpec((GROUP * HD, BLOCK), lambda h: (h, 0))
    return pl.pallas_call(
        near_forward_kernel,
        grid=(HALF,),
        in_specs=[wide, wide, key, value],
        out_specs=[tall, pl.BlockSpec((8, BLOCK), lambda h: (h, 0)), tall],
        out_shape=[
            jax.ShapeDtypeStruct(queries.shape[::-1], f32),
            jax.ShapeDtypeStruct((HALF * 8, BLOCK), f32),
            jax.ShapeDtypeStruct(queries.shape[::-1], bf16),
        ],
        scratch_shapes=[pltpu.VMEM((HD, BLOCK), bf16)],
        compiler_params=pltpu.CompilerParams(vmem_limit_bytes=60 * 2**20),
        cost_estimate=cost(HALF, BLOCK * 3 // 4, 2),
        name="near_forward",
    )(queries, cot, near, near)


def far_kernel(
    chosen, queries, cot_t, near_t, lse_t, far, att_t, grad_t, stats, grad_far, keys_t, values_t, sum_k, sum_v
):
    h = pl.program_id(0)
    first = chosen[2 * h]
    second = chosen[2 * h + 1]
    keys_t[...] = far[:, 0, 0].reshape(FAR, HD).T
    values_t[...] = far[:, 0, 1].reshape(FAR, HD).T

    def one(g, masked, general):
        k = far[:, 0, 0].reshape(FAR, HD)
        v = far[:, 0, 1].reshape(FAR, HD)
        cols = pl.ds(g * HD if isinstance(g, int) else pl.multiple_of(g * HD, HD), HD)
        q = queries[:, cols]
        l0 = lse_t[pl.ds(g, 1), :]
        score = dot(k, q, NT) * SCALE_LOG2
        if masked:
            row = lax.broadcasted_iota(jnp.int32, score.shape, 0)
            entry = jnp.where(jnp.bitwise_and(row, 8) == 0, first, second)
            score = jnp.where(entry < 0, -1e30, score)
        top = jnp.maximum(jnp.max(score, axis=0, keepdims=True), l0) if general else l0
        raised = jnp.exp2(score - top)
        near = jnp.exp2(l0 - top) if general else 1.0
        total = jnp.sum(raised, axis=0, keepdims=True) + near
        over = 1.0 / total
        raised_b = raised.astype(bf16)
        out = (dot(values_t[...], raised_b, NN) + near * near_t[cols, :]) * over
        att_t[cols, :] = out.astype(bf16)
        cot_over = (cot_t[cols, :].astype(f32) * over).astype(bf16)
        delta = jnp.sum(cot_over.astype(f32) * out, axis=0, keepdims=True)
        dscore = (raised * (dot(v, cot_over, NN) - delta)).astype(bf16)
        grad_t[cols, :] = dot(keys_t[...], dscore, NN)
        sum_v[...] += dot(raised_b, cot_over, NT)
        sum_k[...] += dot(dscore, q, NN)
        stats[pl.ds(g, 1), :] = top + jnp.log2(total)
        stats[pl.ds(GROUP + g, 1), :] = delta * total
        return total

    def run(masked):
        worst = jnp.zeros((1, BLOCK), f32)
        for g in range(GROUP):
            worst = jnp.maximum(worst, one(g, masked, False))
        return jnp.max(worst)

    def clear():
        sum_k[...] = jnp.zeros_like(sum_k)
        sum_v[...] = jnp.zeros_like(sum_v)

    clear()
    alive = jnp.minimum(first, second) >= 0
    worst = lax.cond(alive, lambda: run(False), lambda: run(True))

    @pl.when(jnp.logical_not(worst <= LIMIT))
    def _():
        def again(g, carry):
            one(g, True, True)
            return carry

        clear()
        lax.fori_loop(0, GROUP, again, 0)

    grad_far[:, 0, 0] = (sum_k[...] * SCALE).astype(bf16).reshape(BLOCKS, 16, HD)
    grad_far[:, 0, 1] = sum_v[...].astype(bf16).reshape(BLOCKS, 16, HD)


def far_attention(chosen, queries, cot_t, near_t, lse_t, far):
    wide = pl.BlockSpec((BLOCK, GROUP * HD), lambda h, c: (0, h))
    tall = pl.BlockSpec((GROUP * HD, BLOCK), lambda h, c: (h, 0))
    rows = pl.BlockSpec((8, BLOCK), lambda h, c: (h, 0))
    gated = pl.BlockSpec((BLOCKS, 1, 2, 16, HD), lambda h, c: (0, h, 0, 0, 0))
    return pl.pallas_call(
        far_kernel,
        grid_spec=pltpu.PrefetchScalarGridSpec(
            num_scalar_prefetch=1,
            grid=(HALF,),
            in_specs=[wide, tall, tall, rows, gated],
            out_specs=[tall, tall, rows, gated],
            scratch_shapes=[pltpu.VMEM((HD, FAR), bf16)] * 2 + [pltpu.VMEM((FAR, HD), f32)] * 2,
        ),
        out_shape=[
            jax.ShapeDtypeStruct(cot_t.shape, bf16),
            jax.ShapeDtypeStruct(cot_t.shape, f32),
            jax.ShapeDtypeStruct(lse_t.shape, f32),
            jax.ShapeDtypeStruct(far.shape, bf16),
        ],
        compiler_params=pltpu.CompilerParams(vmem_limit_bytes=60 * 2**20),
        cost_estimate=cost(HALF, FAR, 6),
        name="far_attention",
    )(chosen, queries, cot_t, near_t, lse_t, far)


def near_backward_kernel(
    queries, cot, keys, values, stats, att_t, far_t, att, grad_q, grad_k, grad_v, keys_t, values_t, sum_k, sum_v
):
    keys_t[...] = keys[...].T
    values_t[...] = values[...].T
    att[...] = att_t[...].T
    sum_k[...] = jnp.zeros_like(sum_k)
    sum_v[...] = jnp.zeros_like(sum_v)
    columns = stats[...].T
    for piece in (0, 1):
        rows = slice(ROWS * piece, ROWS * piece + ROWS)
        width = ROWS * piece + ROWS
        for g in range(GROUP):
            cols = slice(HD * g, HD * g + HD)
            q = queries[rows, cols]
            c = cot[rows, cols]
            score = near_scores(q, keys_t[:, :width], piece)
            weight = jnp.exp2(score - columns[rows, g : g + 1])
            dweight = dot(c, values_t[:, :width], NN)
            dscore = (weight * (dweight - columns[rows, GROUP + g : GROUP + g + 1])).astype(bf16)
            grad = far_t[cols, rows].T + dot(dscore, keys[:width], NN)
            grad_q[rows, cols] = (grad * SCALE).astype(bf16)
            sum_v[:, :width] += dot(c, weight.astype(bf16), TN)
            sum_k[:, :width] += dot(q, dscore, TN)
    grad_k[...] = sum_k[...].T * SCALE
    grad_v[...] = sum_v[...].T


def near_backward(queries, cot, near, stats, att_t, far_t):
    wide = pl.BlockSpec((BLOCK, GROUP * HD), lambda h: (0, h))
    tall = pl.BlockSpec((GROUP * HD, BLOCK), lambda h: (h, 0))
    key = pl.BlockSpec((BLOCK, HD), lambda h: (0, h))
    value = pl.BlockSpec((BLOCK, HD), lambda h: (0, HALF + h))
    return pl.pallas_call(
        near_backward_kernel,
        grid=(HALF,),
        in_specs=[wide, wide, key, value, pl.BlockSpec((8, BLOCK), lambda h: (h, 0)), tall, tall],
        out_specs=[wide, wide, key, key],
        out_shape=[jax.ShapeDtypeStruct(queries.shape, bf16)] * 2
        + [jax.ShapeDtypeStruct((BLOCK, HALF * HD), f32)] * 2,
        scratch_shapes=[pltpu.VMEM((HD, BLOCK), bf16)] * 2 + [pltpu.VMEM((HD, BLOCK), f32)] * 2,
        compiler_params=pltpu.CompilerParams(vmem_limit_bytes=58 * 2**20),
        cost_estimate=cost(HALF, BLOCK * 3 // 4, 5),
        name="near_backward",
    )(queries, cot, near, near, stats, att_t, far_t)


def spread(x):
    return lax.all_to_all(x, "ctx", 0, 0, axis_index_groups=SAME_HALF, tiled=True)


def halves(x, core):
    width = x.shape[1] // 2
    mine = lax.dynamic_slice_in_dim(x, core * width, width, 1)
    return mine, lax.dynamic_slice_in_dim(x, (1 - core) * width, width, 1)


def swap(x):
    return lax.ppermute(x, "ctx", PAIR)


def in_order(mine, other, core, axis):
    return jnp.where(
        core == 0,
        jnp.concatenate([mine, other], axis=axis),
        jnp.concatenate([other, mine], axis=axis),
    )


def to_block(x, core):
    mine, other = halves(x, core)
    return in_order(mine, swap(other), core, 0)


def others_rows(x, core):
    half = x.shape[0] // 2
    return lax.dynamic_slice_in_dim(x, (1 - core) * half, half, 0)


def my_rows(x, core):
    half = x.shape[0] // 2
    return lax.dynamic_slice_in_dim(x, core * half, half, 0)


def per_device(queries, keys, values, cotangent, selected):
    core = lax.axis_index("ctx") % 2
    my_keys, other_keys = halves(keys, core)
    my_values, other_values = halves(values, core)
    near = in_order(
        jnp.concatenate([my_keys, my_values], axis=1),
        swap(jnp.concatenate([other_keys, other_values], axis=1)),
        core,
        0,
    )
    tiles = jnp.transpose(near.reshape(BLOCKS, 8, 2 * HALF, HD), (0, 2, 1, 3))
    row = jnp.pad(selected.astype(bf16), ((0, 7), (0, HD - selected.shape[1])))
    row = jnp.broadcast_to(row[None, None], (BLOCKS, 1, 8, HD))
    tiles = jnp.concatenate([tiles, row], axis=1)
    shares = spread(tiles)
    table = shares[:, -1, 0, : 2 * KVH].astype(jnp.int32)
    table = jnp.where(core == 0, table[:, :KVH], table[:, KVH:]).reshape(-1)
    chosen = jnp.where(core == 0, selected[0, :KVH], selected[0, KVH:])
    picked = pick(table, shares)
    picked, queries, cotangent = lax.optimization_barrier((picked, queries, cotangent))
    far = spread(picked)
    block_queries = to_block(queries, core)
    block_cot = to_block(cotangent, core)
    near_t, lse_t, cot_t = near_forward(block_queries, block_cot, near)
    far, near_t, lse_t, cot_t = lax.optimization_barrier((far, near_t, lse_t, cot_t))
    att_t, far_t, stats, grad_far = far_attention(
        chosen, block_queries, cot_t, near_t, lse_t, far
    )
    back = spread(grad_far)
    attended, grad_q, grad_k, grad_v = near_backward(
        block_queries, block_cot, near, stats, att_t, far_t
    )
    near_other = swap(
        jnp.concatenate([others_rows(x, core).astype(bf16) for x in (grad_k, grad_v)], axis=1)
    )
    other_attended = swap(others_rows(attended, core))
    other_q = swap(others_rows(grad_q, core))
    back, grad_k, grad_v, near_other, attended, grad_q, other_attended, other_q = (
        lax.optimization_barrier(
            (back, grad_k, grad_v, near_other, attended, grad_q, other_attended, other_q)
        )
    )
    summed = spread(add_terms(table, back))
    attended = in_order(my_rows(attended, core), other_attended, core, 1)
    grad_q = in_order(my_rows(grad_q, core), other_q, core, 1)
    summed, attended, grad_q = lax.optimization_barrier((summed, attended, grad_q))
    other = swap(others_rows(summed, core))
    grad_k, grad_v = finish(core, summed, other, grad_k, grad_v, near_other)
    return attended, grad_q, grad_k, grad_v


def solution(mesh):
    specs = (P("ctx", None),) * 5
    return jax.shard_map(
        per_device, mesh=mesh, in_specs=specs, out_specs=specs[:4], check_vma=False
    )
```

```python
import math

import jax
import jax.numpy as jnp
from jax import lax
from jax.experimental import pallas as pl
from jax.experimental.pallas import tpu as pltpu
from jax.sharding import PartitionSpec as P

HD = 128
QH = 32
KVH = 8
BLOCK = 512
ROWS = 256
BLOCKS = 64
HALF = KVH // 2
GROUP = QH // KVH
FAR = 2 * BLOCK
SCALE = HD ** -0.5
SCALE_LOG2 = SCALE * math.log2(math.e)
NN = (((1,), (0,)), ((), ()))
NT = (((1,), (1,)), ((), ()))
TN = (((0,), (0,)), ((), ()))
f32 = jnp.float32
bf16 = jnp.bfloat16
LIMIT = 2.0**40

PAIR = [(i, i ^ 1) for i in range(2 * BLOCKS)]
SAME_HALF = [list(range(k, 2 * BLOCKS, 2)) for k in (0, 1)]


def pick_kernel(table, shares, out):
    step = pl.program_id(0)
    count, heads = out.shape[:2]

    def one(i, carry):
        row = (step * count + i) * 2 * heads
        for h in range(heads):
            first = jnp.maximum(table[row + 2 * h], 0)
            second = jnp.maximum(table[row + 2 * h + 1], 0)
            for kv in range(2):
                tile = kv * HALF + h
                out[i, h, kv, :8] = shares[first, tile]
                out[i, h, kv, 8:] = shares[second, tile]
        return carry

    lax.fori_loop(0, count, one, 0, unroll=8)


def pick(table, shares):
    count = 32
    return pl.pallas_call(
        pick_kernel,
        grid_spec=pltpu.PrefetchScalarGridSpec(
            num_scalar_prefetch=1,
            grid=(BLOCKS // count,),
            in_specs=[pl.BlockSpec(shares.shape, lambda i, t: (0, 0, 0, 0))],
            out_specs=pl.BlockSpec((count, HALF, 2, 16, HD), lambda i, t: (i, 0, 0, 0, 0)),
        ),
        out_shape=jax.ShapeDtypeStruct((BLOCKS, HALF, 2, 16, HD), bf16),
        compiler_params=pltpu.CompilerParams(vmem_limit_bytes=16 * 2**20),
        name="pick",
    )(table, shares)


def add_kernel(table, terms, out, total):
    step = pl.program_id(0)
    count, heads = terms.shape[:2]

    @pl.when(step == 0)
    def _():
        total[...] = jnp.zeros_like(total)

    def one(i, carry):
        row = (step * count + i) * 2 * heads
        places = []
        sums = []
        for h in range(heads):
            for e in range(2):
                block = table[row + 2 * h + e]
                slot = jnp.where(block < 0, BLOCKS, block)
                for kv in range(2):
                    place = (slot, kv * heads + h)
                    term = terms[i, h, kv].astype(f32)[8 * e : 8 * e + 8]
                    places.append(place)
                    sums.append(total[place] + term)
        for place, value in zip(places, sums):
            total[place] = value
        return carry

    lax.fori_loop(0, count, one, 0, unroll=8)

    @pl.when(step == pl.num_programs(0) - 1)
    def _():
        out[...] = total[:BLOCKS].astype(bf16)


def add_terms(table, terms):
    count = 16
    tiles = 2 * terms.shape[1]
    whole = lambda i, t: (0, 0, 0, 0)
    return pl.pallas_call(
        add_kernel,
        grid_spec=pltpu.PrefetchScalarGridSpec(
            num_scalar_prefetch=1,
            grid=(BLOCKS // count,),
            in_specs=[pl.BlockSpec((count,) + terms.shape[1:], lambda i, t: (i, 0, 0, 0, 0))],
            out_specs=pl.BlockSpec((BLOCKS, tiles, 8, HD), whole),
            scratch_shapes=[pltpu.VMEM((BLOCKS + 1, tiles, 8, HD), f32)],
        ),
        out_shape=jax.ShapeDtypeStruct((BLOCKS, tiles, 8, HD), bf16),
        compiler_params=pltpu.CompilerParams(vmem_limit_bytes=16 * 2**20),
        name="add_terms",
    )(table, terms)


def finish_kernel(core, mine, other, near_k, near_v, near_other, grad_k, grad_v):
    rows = grad_k.shape[0]
    for side, far in ((core[0], mine), (1 - core[0], other)):
        for kv, (out, near) in enumerate(((grad_k, near_k), (grad_v, near_v))):
            for h in range(HALF):
                tile = kv * HALF + h
                term = far[:, tile].reshape(rows, HD).astype(f32)
                if far is mine:
                    term += near[:, HD * h : HD * h + HD]
                else:
                    term += near_other[:, HD * tile : HD * tile + HD].astype(f32)
                place = pl.ds(pl.multiple_of((side * HALF + h) * HD, HD), HD)
                out[:, place] = term.astype(bf16)


def finish(core, mine, other, near_k, near_v, near_other):
    steps = 2
    tiles = mine.shape[1]
    chunk = ROWS // 8 // steps
    far = pl.BlockSpec((chunk, tiles, 8, HD), lambda i, c: (i, 0, 0, 0))
    far_mine = pl.BlockSpec((chunk, tiles, 8, HD), lambda i, c: (i + steps * c[0], 0, 0, 0))
    rows = pl.BlockSpec((ROWS // steps, KVH * HD), lambda i, c: (i, 0))
    rows_mine = pl.BlockSpec((ROWS // steps, HALF * HD), lambda i, c: (i + steps * c[0], 0))
    return pl.pallas_call(
        finish_kernel,
        grid_spec=pltpu.PrefetchScalarGridSpec(
            num_scalar_prefetch=1,
            grid=(steps,),
            in_specs=[far_mine, far, rows_mine, rows_mine, rows],
            out_specs=[rows, rows],
        ),
        out_shape=[jax.ShapeDtypeStruct((ROWS, KVH * HD), bf16)] * 2,
        compiler_params=pltpu.CompilerParams(vmem_limit_bytes=12 * 2**20),
        name="finish",
    )(core.reshape(1), mine, other, near_k, near_v, near_other)


def dot(a, b, dims):
    return lax.dot_general(a, b, dims, preferred_element_type=f32)


def cost(heads, keys, products):
    pairs = heads * GROUP * BLOCK * keys
    return pl.CostEstimate(
        flops=products * 4 * pairs * HD, transcendentals=pairs, bytes_accessed=heads * 5 * 2**20
    )


def lanes(values):
    each = HD // len(values)
    lane = lax.broadcasted_iota(jnp.int32, (ROWS, HD), 1)
    out = jnp.broadcast_to(values[-1], (ROWS, HD))
    for i in range(len(values) - 2, -1, -1):
        out = jnp.where(lane < (i + 1) * each, values[i], out)
    return out


def near_scores(q, keys_t, piece):
    score = dot(q, keys_t, NN) * SCALE_LOG2
    shape = (ROWS, ROWS)
    causal = lax.broadcasted_iota(jnp.int32, shape, 0) >= lax.broadcasted_iota(jnp.int32, shape, 1)
    diagonal = jnp.where(causal, score[:, ROWS * piece :], -1e30)
    return jnp.concatenate([score[:, :ROWS], diagonal], axis=1) if piece else diagonal


def near_forward_kernel(
    core, my_q, got_q, my_cot, got_cot, keys, values, out_t, lse_t, queries, cot_t, cot, keys_t
):
    for side in (0, 1):
        mine = slice(ROWS * side, ROWS * side + ROWS)
        other = slice(ROWS - ROWS * side, 2 * ROWS - ROWS * side)

        @pl.when(core[0] == side)
        def _():
            queries[mine] = my_q[...]
            queries[other] = got_q[...]
            cot[mine] = my_cot[...]
            cot[other] = got_cot[...]

    keys_t[...] = keys[...].T
    cot_t[...] = cot[...].T
    for piece in (0, 1):
        rows = slice(ROWS * piece, ROWS * piece + ROWS)
        width = ROWS * piece + ROWS
        found = []
        for g in range(GROUP):
            cols = slice(HD * g, HD * g + HD)
            score = near_scores(queries[rows, cols], keys_t[:, :width], piece)
            top = jnp.max(score, axis=1, keepdims=True)
            raised = jnp.exp2(score - top)
            total = jnp.sum(raised, axis=1, keepdims=True)
            out = dot(raised.astype(bf16), values[:width], NN) * (1.0 / total)
            out_t[cols, rows] = out.T.astype(out_t.dtype)
            found.append(top + jnp.log2(total))
        lse = lanes(found).T
        for g in range(GROUP):
            lse_t[g : g + 1, rows] = lse[HD // GROUP * g : HD // GROUP * g + 1]


def near_forward(core, my_q, got_q, my_cot, got_cot, near):
    mine = pl.BlockSpec((ROWS, GROUP * HD), lambda h, c: (0, HALF * c[0] + h))
    got = pl.BlockSpec((ROWS, GROUP * HD), lambda h, c: (0, h))
    wide = pl.BlockSpec((BLOCK, GROUP * HD), lambda h, c: (0, h))
    key = pl.BlockSpec((BLOCK, HD), lambda h, c: (0, h))
    value = pl.BlockSpec((BLOCK, HD), lambda h, c: (0, HALF + h))
    tall = pl.BlockSpec((GROUP * HD, BLOCK), lambda h, c: (h, 0))
    width = HALF * GROUP * HD
    return pl.pallas_call(
        near_forward_kernel,
        grid_spec=pltpu.PrefetchScalarGridSpec(
            num_scalar_prefetch=1,
            grid=(HALF,),
            in_specs=[mine, got, mine, got, key, value],
            out_specs=[tall, pl.BlockSpec((8, BLOCK), lambda h, c: (h, 0)), wide, tall],
            scratch_shapes=[pltpu.VMEM((BLOCK, GROUP * HD), bf16), pltpu.VMEM((HD, BLOCK), bf16)],
        ),
        out_shape=[
            jax.ShapeDtypeStruct((width, BLOCK), f32),
            jax.ShapeDtypeStruct((HALF * 8, BLOCK), f32),
            jax.ShapeDtypeStruct((BLOCK, width), bf16),
            jax.ShapeDtypeStruct((width, BLOCK), bf16),
        ],
        compiler_params=pltpu.CompilerParams(vmem_limit_bytes=62 * 2**20),
        cost_estimate=cost(HALF, BLOCK * 3 // 4, 2),
        name="near_forward",
    )(core.reshape(1), my_q, got_q, my_cot, got_cot, near, near)


def far_kernel(
    chosen, queries, cot_t, near_t, lse_t, far, att_t, grad_t, stats, grad_far, keys_t, values_t, sum_k, sum_v
):
    h = pl.program_id(0)
    first = chosen[2 * h]
    second = chosen[2 * h + 1]
    keys_t[...] = far[:, 0, 0].reshape(FAR, HD).T
    values_t[...] = far[:, 0, 1].reshape(FAR, HD).T

    def one(g, masked, general):
        k = far[:, 0, 0].reshape(FAR, HD)
        v = far[:, 0, 1].reshape(FAR, HD)
        cols = pl.ds(g * HD if isinstance(g, int) else pl.multiple_of(g * HD, HD), HD)
        q = queries[:, cols]
        l0 = lse_t[pl.ds(g, 1), :]
        score = dot(k, q, NT) * SCALE_LOG2
        if masked:
            row = lax.broadcasted_iota(jnp.int32, score.shape, 0)
            entry = jnp.where(jnp.bitwise_and(row, 8) == 0, first, second)
            score = jnp.where(entry < 0, -1e30, score)
        top = jnp.maximum(jnp.max(score, axis=0, keepdims=True), l0) if general else l0
        raised = jnp.exp2(score - top)
        near = jnp.exp2(l0 - top) if general else 1.0
        total = jnp.sum(raised, axis=0, keepdims=True) + near
        over = 1.0 / total
        raised_b = raised.astype(bf16)
        out = (dot(values_t[...], raised_b, NN) + near * near_t[cols, :].astype(f32)) * over
        att_t[cols, :] = out.astype(bf16)
        cot_over = (cot_t[cols, :].astype(f32) * over).astype(bf16)
        delta = jnp.sum(cot_over.astype(f32) * out, axis=0, keepdims=True)
        dscore = (raised * (dot(v, cot_over, NN) - delta)).astype(bf16)
        grad_t[cols, :] = dot(keys_t[...], dscore, NN).astype(grad_t.dtype)
        sum_v[...] += dot(raised_b, cot_over, NT)
        sum_k[...] += dot(dscore, q, NN)
        stats[pl.ds(g, 1), :] = top + jnp.log2(total)
        stats[pl.ds(GROUP + g, 1), :] = delta * total
        return total

    def run(masked):
        worst = jnp.zeros((1, BLOCK), f32)
        for g in range(GROUP):
            worst = jnp.maximum(worst, one(g, masked, False))
        return jnp.max(worst)

    def clear():
        sum_k[...] = jnp.zeros_like(sum_k)
        sum_v[...] = jnp.zeros_like(sum_v)

    clear()
    alive = jnp.minimum(first, second) >= 0
    worst = lax.cond(alive, lambda: run(False), lambda: run(True))

    @pl.when(jnp.logical_not(worst <= LIMIT))
    def _():
        def again(g, carry):
            one(g, True, True)
            return carry

        clear()
        lax.fori_loop(0, GROUP, again, 0)

    grad_far[:, 0, 0] = (sum_k[...] * SCALE).astype(bf16).reshape(BLOCKS, 16, HD)
    grad_far[:, 0, 1] = sum_v[...].astype(bf16).reshape(BLOCKS, 16, HD)


def far_attention(chosen, queries, cot_t, near_t, lse_t, far):
    wide = pl.BlockSpec((BLOCK, GROUP * HD), lambda h, c: (0, h))
    tall = pl.BlockSpec((GROUP * HD, BLOCK), lambda h, c: (h, 0))
    rows = pl.BlockSpec((8, BLOCK), lambda h, c: (h, 0))
    gated = pl.BlockSpec((BLOCKS, 1, 2, 16, HD), lambda h, c: (0, h, 0, 0, 0))
    return pl.pallas_call(
        far_kernel,
        grid_spec=pltpu.PrefetchScalarGridSpec(
            num_scalar_prefetch=1,
            grid=(HALF,),
            in_specs=[wide, tall, tall, rows, gated],
            out_specs=[tall, tall, rows, gated],
            scratch_shapes=[pltpu.VMEM((HD, FAR), bf16)] * 2 + [pltpu.VMEM((FAR, HD), f32)] * 2,
        ),
        out_shape=[
            jax.ShapeDtypeStruct(cot_t.shape, bf16),
            jax.ShapeDtypeStruct(cot_t.shape, f32),
            jax.ShapeDtypeStruct(lse_t.shape, f32),
            jax.ShapeDtypeStruct(far.shape, bf16),
        ],
        compiler_params=pltpu.CompilerParams(vmem_limit_bytes=60 * 2**20),
        cost_estimate=cost(HALF, FAR, 6),
        name="far_attention",
    )(chosen, queries, cot_t, near_t, lse_t, far)


def near_backward_kernel(
    queries, cot_t, keys, values, stats, att_t, far_t, att, grad_q, grad_k, grad_v, keys_t, values_t, sum_k, sum_v
):
    keys_t[...] = keys[...].T
    values_t[...] = values[...].T
    att[...] = att_t[...].T
    sum_k[...] = jnp.zeros_like(sum_k)
    sum_v[...] = jnp.zeros_like(sum_v)
    columns = stats[...].T
    for piece in (0, 1):
        rows = slice(ROWS * piece, ROWS * piece + ROWS)
        width = ROWS * piece + ROWS
        for g in range(GROUP):
            cols = slice(HD * g, HD * g + HD)
            q = queries[rows, cols]
            c = cot_t[cols, rows]
            score = near_scores(q, keys_t[:, :width], piece)
            weight = jnp.exp2(score - columns[rows, g : g + 1])
            dweight = dot(c, values_t[:, :width], TN)
            dscore = (weight * (dweight - columns[rows, GROUP + g : GROUP + g + 1])).astype(bf16)
            grad = far_t[cols, rows].astype(f32).T + dot(dscore, keys[:width], NN)
            grad_q[rows, cols] = (grad * SCALE).astype(bf16)
            sum_v[:, :width] += dot(c, weight.astype(bf16), NN)
            sum_k[:, :width] += dot(q, dscore, TN)
    grad_k[...] = sum_k[...].T * SCALE
    grad_v[...] = sum_v[...].T


def near_backward(queries, cot_t, near, stats, att_t, far_t):
    wide = pl.BlockSpec((BLOCK, GROUP * HD), lambda h: (0, h))
    tall = pl.BlockSpec((GROUP * HD, BLOCK), lambda h: (h, 0))
    key = pl.BlockSpec((BLOCK, HD), lambda h: (0, h))
    value = pl.BlockSpec((BLOCK, HD), lambda h: (0, HALF + h))
    return pl.pallas_call(
        near_backward_kernel,
        grid=(HALF,),
        in_specs=[wide, tall, key, value, pl.BlockSpec((8, BLOCK), lambda h: (h, 0)), tall, tall],
        out_specs=[wide, wide, key, key],
        out_shape=[jax.ShapeDtypeStruct(queries.shape, bf16)] * 2
        + [jax.ShapeDtypeStruct((BLOCK, HALF * HD), f32)] * 2,
        scratch_shapes=[pltpu.VMEM((HD, BLOCK), bf16)] * 2 + [pltpu.VMEM((HD, BLOCK), f32)] * 2,
        compiler_params=pltpu.CompilerParams(vmem_limit_bytes=58 * 2**20),
        cost_estimate=cost(HALF, BLOCK * 3 // 4, 5),
        name="near_backward",
    )(queries, cot_t, near, near, stats, att_t, far_t)


def spread(x):
    return lax.all_to_all(x, "ctx", 0, 0, axis_index_groups=SAME_HALF, tiled=True)


def halves(x, core):
    width = x.shape[1] // 2
    mine = lax.dynamic_slice_in_dim(x, core * width, width, 1)
    return mine, lax.dynamic_slice_in_dim(x, (1 - core) * width, width, 1)


def swap(x):
    return lax.ppermute(x, "ctx", PAIR)


def in_order(mine, other, core, axis):
    return jnp.where(
        core == 0,
        jnp.concatenate([mine, other], axis=axis),
        jnp.concatenate([other, mine], axis=axis),
    )


def others_rows(x, core):
    half = x.shape[0] // 2
    return lax.dynamic_slice_in_dim(x, (1 - core) * half, half, 0)


def my_rows(x, core):
    half = x.shape[0] // 2
    return lax.dynamic_slice_in_dim(x, core * half, half, 0)


def per_device(queries, keys, values, cotangent, selected):
    core = lax.axis_index("ctx") % 2
    my_keys, other_keys = halves(keys, core)
    my_values, other_values = halves(values, core)
    near = in_order(
        jnp.concatenate([my_keys, my_values], axis=1),
        swap(jnp.concatenate([other_keys, other_values], axis=1)),
        core,
        0,
    )
    tiles = jnp.transpose(near.reshape(BLOCKS, 8, 2 * HALF, HD), (0, 2, 1, 3))
    row = jnp.pad(selected.astype(bf16), ((0, 7), (0, HD - selected.shape[1])))
    row = jnp.broadcast_to(row[None, None], (BLOCKS, 1, 8, HD))
    tiles = jnp.concatenate([tiles, row], axis=1)
    shares = spread(tiles)
    table = shares[:, -1, 0, : 2 * KVH].astype(jnp.int32)
    table = jnp.where(core == 0, table[:, :KVH], table[:, KVH:]).reshape(-1)
    chosen = jnp.where(core == 0, selected[0, :KVH], selected[0, KVH:])
    picked = pick(table, shares)
    picked, queries, cotangent = lax.optimization_barrier((picked, queries, cotangent))
    far = spread(picked)
    got_q = swap(halves(queries, core)[1])
    got_cot = swap(halves(cotangent, core)[1])
    near_t, lse_t, block_q, cot_t = near_forward(core, queries, got_q, cotangent, got_cot, near)
    far, near_t, lse_t, cot_t = lax.optimization_barrier((far, near_t, lse_t, cot_t))
    att_t, far_t, stats, grad_far = far_attention(
        chosen, block_q, cot_t, near_t, lse_t, far
    )
    back = spread(grad_far)
    attended, grad_q, grad_k, grad_v = near_backward(block_q, cot_t, near, stats, att_t, far_t)
    near_other = swap(
        jnp.concatenate([others_rows(x, core).astype(bf16) for x in (grad_k, grad_v)], axis=1)
    )
    other_attended = swap(others_rows(attended, core))
    other_q = swap(others_rows(grad_q, core))
    back, grad_k, grad_v, near_other, attended, grad_q, other_attended, other_q = (
        lax.optimization_barrier(
            (back, grad_k, grad_v, near_other, attended, grad_q, other_attended, other_q)
        )
    )
    summed = spread(add_terms(table, back))
    attended = in_order(my_rows(attended, core), other_attended, core, 1)
    grad_q = in_order(my_rows(grad_q, core), other_q, core, 1)
    summed, attended, grad_q = lax.optimization_barrier((summed, attended, grad_q))
    other = swap(others_rows(summed, core))
    grad_k, grad_v = finish(core, summed, other, grad_k, grad_v, near_other)
    return attended, grad_q, grad_k, grad_v


def solution(mesh):
    specs = (P("ctx", None),) * 5
    return jax.shard_map(
        per_device, mesh=mesh, in_specs=specs, out_specs=specs[:4], check_vma=False
    )
```

```python
import math

import jax
import jax.numpy as jnp
from jax import lax
from jax.experimental import pallas as pl
from jax.experimental.pallas import tpu as pltpu
from jax.sharding import PartitionSpec as P

HD = 128
QH = 32
KVH = 8
BLOCK = 512
ROWS = 256
BLOCKS = 64
HALF = KVH // 2
GROUP = QH // KVH
FAR = 2 * BLOCK
SCALE = HD ** -0.5
SCALE_LOG2 = SCALE * math.log2(math.e)
NN = (((1,), (0,)), ((), ()))
NT = (((1,), (1,)), ((), ()))
TN = (((0,), (0,)), ((), ()))
f32 = jnp.float32
bf16 = jnp.bfloat16
LIMIT = 2.0**40

PAIR = [(i, i ^ 1) for i in range(2 * BLOCKS)]
SAME_HALF = [list(range(k, 2 * BLOCKS, 2)) for k in (0, 1)]


def pick_kernel(table, shares, out):
    step = pl.program_id(0)
    count, heads = out.shape[:2]

    def one(i, carry):
        row = (step * count + i) * 2 * heads
        for h in range(heads):
            first = jnp.maximum(table[row + 2 * h], 0)
            second = jnp.maximum(table[row + 2 * h + 1], 0)
            for kv in range(2):
                tile = kv * HALF + h
                out[i, h, kv] = jnp.concatenate([shares[first, tile], shares[second, tile]], axis=0)
        return carry

    lax.fori_loop(0, count, one, 0, unroll=8)


def pick(table, shares):
    count = 32
    return pl.pallas_call(
        pick_kernel,
        grid_spec=pltpu.PrefetchScalarGridSpec(
            num_scalar_prefetch=1,
            grid=(BLOCKS // count,),
            in_specs=[pl.BlockSpec(shares.shape, lambda i, t: (0, 0, 0, 0))],
            out_specs=pl.BlockSpec((count, HALF, 2, 16, HD), lambda i, t: (i, 0, 0, 0, 0)),
        ),
        out_shape=jax.ShapeDtypeStruct((BLOCKS, HALF, 2, 16, HD), bf16),
        compiler_params=pltpu.CompilerParams(vmem_limit_bytes=16 * 2**20),
        name="pick",
    )(table, shares)


def add_kernel(table, terms, out, total):
    step = pl.program_id(0)
    count, heads = terms.shape[:2]

    @pl.when(step == 0)
    def _():
        total[...] = jnp.zeros_like(total)

    def one(i, carry):
        row = (step * count + i) * 2 * heads
        places = []
        sums = []
        for h in range(heads):
            for e in range(2):
                block = table[row + 2 * h + e]
                slot = jnp.where(block < 0, BLOCKS, block)
                for kv in range(2):
                    place = (slot, kv * heads + h)
                    term = terms[i, h, kv].astype(f32)[8 * e : 8 * e + 8]
                    places.append(place)
                    sums.append(total[place] + term)
        for place, value in zip(places, sums):
            total[place] = value
        return carry

    lax.fori_loop(0, count, one, 0, unroll=8)

    @pl.when(step == pl.num_programs(0) - 1)
    def _():
        out[...] = total[:BLOCKS].astype(bf16)


def add_terms(table, terms):
    count = 16
    tiles = 2 * terms.shape[1]
    whole = lambda i, t: (0, 0, 0, 0)
    return pl.pallas_call(
        add_kernel,
        grid_spec=pltpu.PrefetchScalarGridSpec(
            num_scalar_prefetch=1,
            grid=(BLOCKS // count,),
            in_specs=[pl.BlockSpec((count,) + terms.shape[1:], lambda i, t: (i, 0, 0, 0, 0))],
            out_specs=pl.BlockSpec((BLOCKS, tiles, 8, HD), whole),
            scratch_shapes=[pltpu.VMEM((BLOCKS + 1, tiles, 8, HD), f32)],
        ),
        out_shape=jax.ShapeDtypeStruct((BLOCKS, tiles, 8, HD), bf16),
        compiler_params=pltpu.CompilerParams(vmem_limit_bytes=16 * 2**20),
        name="add_terms",
    )(table, terms)


def finish_kernel(core, mine, other, near_k, near_v, near_other, grad_k, grad_v):
    rows = grad_k.shape[0]
    for side, far in ((core[0], mine), (1 - core[0], other)):
        for kv, (out, near) in enumerate(((grad_k, near_k), (grad_v, near_v))):
            for h in range(HALF):
                tile = kv * HALF + h
                term = far[:, tile].astype(f32).reshape(rows, HD)
                if far is mine:
                    term += near[:, HD * h : HD * h + HD]
                else:
                    term += near_other[kv, :, HD * h : HD * h + HD].astype(f32)
                place = pl.ds(pl.multiple_of((side * HALF + h) * HD, HD), HD)
                out[:, place] = term.astype(bf16)


def finish(core, mine, other, near_k, near_v, near_other):
    steps = 2
    tiles = mine.shape[1]
    chunk = ROWS // 8 // steps
    far = pl.BlockSpec((chunk, tiles, 8, HD), lambda i, c: (i, 0, 0, 0))
    far_mine = pl.BlockSpec((chunk, tiles, 8, HD), lambda i, c: (i + steps * c[0], 0, 0, 0))
    rows = pl.BlockSpec((ROWS // steps, KVH * HD), lambda i, c: (i, 0))
    rows_mine = pl.BlockSpec((ROWS // steps, HALF * HD), lambda i, c: (i + steps * c[0], 0))
    return pl.pallas_call(
        finish_kernel,
        grid_spec=pltpu.PrefetchScalarGridSpec(
            num_scalar_prefetch=1,
            grid=(steps,),
            in_specs=[
                far_mine,
                far,
                rows_mine,
                rows_mine,
                pl.BlockSpec((2, ROWS // steps, HALF * HD), lambda i, c: (0, i, 0)),
            ],
            out_specs=[rows, rows],
        ),
        out_shape=[jax.ShapeDtypeStruct((ROWS, KVH * HD), bf16)] * 2,
        compiler_params=pltpu.CompilerParams(vmem_limit_bytes=12 * 2**20),
        name="finish",
    )(core.reshape(1), mine, other, near_k, near_v, near_other)


def dot(a, b, dims):
    return lax.dot_general(a, b, dims, preferred_element_type=f32)


def cost(heads, keys, products):
    pairs = heads * GROUP * BLOCK * keys
    return pl.CostEstimate(
        flops=products * 4 * pairs * HD, transcendentals=pairs, bytes_accessed=heads * 5 * 2**20
    )


def lanes(values):
    each = HD // len(values)
    lane = lax.broadcasted_iota(jnp.int32, (ROWS, HD), 1)
    out = jnp.broadcast_to(values[-1], (ROWS, HD))
    for i in range(len(values) - 2, -1, -1):
        out = jnp.where(lane < (i + 1) * each, values[i], out)
    return out


def near_scores(q, keys_t, piece):
    score = dot(q, keys_t, NN) * SCALE_LOG2
    shape = (ROWS, ROWS)
    causal = lax.broadcasted_iota(jnp.int32, shape, 0) >= lax.broadcasted_iota(jnp.int32, shape, 1)
    diagonal = jnp.where(causal, score[:, ROWS * piece :], -1e30)
    return jnp.concatenate([score[:, :ROWS], diagonal], axis=1) if piece else diagonal


def near_forward_kernel(
    core, my_q, got_q, my_cot, got_cot, keys, values, out_t, lse_t, queries, cot_t, cot, keys_t
):
    for side in (0, 1):
        mine = slice(ROWS * side, ROWS * side + ROWS)
        other = slice(ROWS - ROWS * side, 2 * ROWS - ROWS * side)

        @pl.when(core[0] == side)
        def _():
            queries[mine] = my_q[...]
            queries[other] = got_q[...]
            cot[mine] = my_cot[...]
            cot[other] = got_cot[...]

    keys_t[...] = keys[...].T
    cot_t[...] = cot[...].T
    for piece in (0, 1):
        rows = slice(ROWS * piece, ROWS * piece + ROWS)
        width = ROWS * piece + ROWS
        found = []
        for g in range(GROUP):
            cols = slice(HD * g, HD * g + HD)
            score = near_scores(queries[rows, cols], keys_t[:, :width], piece)
            top = jnp.max(score, axis=1, keepdims=True)
            raised = jnp.exp2(score - top)
            total = jnp.sum(raised, axis=1, keepdims=True)
            out = dot(raised.astype(bf16), values[:width], NN) * (1.0 / total)
            out_t[cols, rows] = out.T.astype(out_t.dtype)
            found.append(top + jnp.log2(total))
        lse = lanes(found).T
        for g in range(GROUP):
            lse_t[g : g + 1, rows] = lse[HD // GROUP * g : HD // GROUP * g + 1]


def near_forward(core, my_q, got_q, my_cot, got_cot, near):
    mine = pl.BlockSpec((ROWS, GROUP * HD), lambda h, c: (0, HALF * c[0] + h))
    got = pl.BlockSpec((ROWS, GROUP * HD), lambda h, c: (0, h))
    wide = pl.BlockSpec((BLOCK, GROUP * HD), lambda h, c: (0, h))
    key = pl.BlockSpec((BLOCK, HD), lambda h, c: (0, h))
    value = pl.BlockSpec((BLOCK, HD), lambda h, c: (0, HALF + h))
    tall = pl.BlockSpec((GROUP * HD, BLOCK), lambda h, c: (h, 0))
    width = HALF * GROUP * HD
    return pl.pallas_call(
        near_forward_kernel,
        grid_spec=pltpu.PrefetchScalarGridSpec(
            num_scalar_prefetch=1,
            grid=(HALF,),
            in_specs=[mine, got, mine, got, key, value],
            out_specs=[tall, pl.BlockSpec((8, BLOCK), lambda h, c: (h, 0)), wide, tall],
            scratch_shapes=[pltpu.VMEM((BLOCK, GROUP * HD), bf16), pltpu.VMEM((HD, BLOCK), bf16)],
        ),
        out_shape=[
            jax.ShapeDtypeStruct((width, BLOCK), f32),
            jax.ShapeDtypeStruct((HALF * 8, BLOCK), f32),
            jax.ShapeDtypeStruct((BLOCK, width), bf16),
            jax.ShapeDtypeStruct((width, BLOCK), bf16),
        ],
        compiler_params=pltpu.CompilerParams(vmem_limit_bytes=62 * 2**20),
        cost_estimate=cost(HALF, BLOCK * 3 // 4, 2),
        name="near_forward",
    )(core.reshape(1), my_q, got_q, my_cot, got_cot, near, near)


def far_kernel(
    chosen, queries, cot_t, near_t, lse_t, far, att_t, grad_t, stats, grad_far, keys_t, values_t, sum_k, sum_v
):
    h = pl.program_id(0)
    first = chosen[2 * h]
    second = chosen[2 * h + 1]
    keys_t[...] = far[:, 0, 0].reshape(FAR, HD).T
    values_t[...] = far[:, 0, 1].reshape(FAR, HD).T

    def one(g, masked, general):
        k = far[:, 0, 0].reshape(FAR, HD)
        v = far[:, 0, 1].reshape(FAR, HD)
        cols = pl.ds(g * HD if isinstance(g, int) else pl.multiple_of(g * HD, HD), HD)
        q = queries[:, cols]
        l0 = lse_t[pl.ds(g, 1), :]
        score = dot(k, q, NT) * SCALE_LOG2
        if masked:
            row = lax.broadcasted_iota(jnp.int32, score.shape, 0)
            entry = jnp.where(jnp.bitwise_and(row, 8) == 0, first, second)
            score = jnp.where(entry < 0, -1e30, score)
        top = jnp.maximum(jnp.max(score, axis=0, keepdims=True), l0) if general else l0
        raised = jnp.exp2(score - top)
        near = jnp.exp2(l0 - top) if general else 1.0
        total = jnp.sum(raised, axis=0, keepdims=True) + near
        over = 1.0 / total
        raised_b = raised.astype(bf16)
        out = (dot(values_t[...], raised_b, NN) + near * near_t[cols, :].astype(f32)) * over
        att_t[cols, :] = out.astype(bf16)
        cot_over = (cot_t[cols, :].astype(f32) * over).astype(bf16)
        delta = jnp.sum(cot_over.astype(f32) * out, axis=0, keepdims=True)
        dscore = (raised * (dot(v, cot_over, NN) - delta)).astype(bf16)
        grad_t[cols, :] = dot(keys_t[...], dscore, NN).astype(grad_t.dtype)
        sum_v[...] += dot(raised_b, cot_over, NT)
        sum_k[...] += dot(dscore, q, NN)
        stats[pl.ds(g, 1), :] = top + jnp.log2(total)
        stats[pl.ds(GROUP + g, 1), :] = delta * total
        return total

    def run(masked):
        worst = jnp.zeros((1, BLOCK), f32)
        for g in range(GROUP):
            worst = jnp.maximum(worst, one(g, masked, False))
        return jnp.max(worst)

    def clear():
        sum_k[...] = jnp.zeros_like(sum_k)
        sum_v[...] = jnp.zeros_like(sum_v)

    clear()
    alive = jnp.minimum(first, second) >= 0
    worst = lax.cond(alive, lambda: run(False), lambda: run(True))

    @pl.when(jnp.logical_not(worst <= LIMIT))
    def _():
        def again(g, carry):
            one(g, True, True)
            return carry

        clear()
        lax.fori_loop(0, GROUP, again, 0)

    grad_far[:, 0, 0] = (sum_k[...] * SCALE).astype(bf16).reshape(BLOCKS, 16, HD)
    grad_far[:, 0, 1] = sum_v[...].astype(bf16).reshape(BLOCKS, 16, HD)


def far_attention(chosen, queries, cot_t, near_t, lse_t, far):
    wide = pl.BlockSpec((BLOCK, GROUP * HD), lambda h, c: (0, h))
    tall = pl.BlockSpec((GROUP * HD, BLOCK), lambda h, c: (h, 0))
    rows = pl.BlockSpec((8, BLOCK), lambda h, c: (h, 0))
    gated = pl.BlockSpec((BLOCKS, 1, 2, 16, HD), lambda h, c: (0, h, 0, 0, 0))
    return pl.pallas_call(
        far_kernel,
        grid_spec=pltpu.PrefetchScalarGridSpec(
            num_scalar_prefetch=1,
            grid=(HALF,),
            in_specs=[wide, tall, tall, rows, gated],
            out_specs=[tall, tall, rows, gated],
            scratch_shapes=[pltpu.VMEM((HD, FAR), bf16)] * 2 + [pltpu.VMEM((FAR, HD), f32)] * 2,
        ),
        out_shape=[
            jax.ShapeDtypeStruct(cot_t.shape, bf16),
            jax.ShapeDtypeStruct(cot_t.shape, f32),
            jax.ShapeDtypeStruct(lse_t.shape, f32),
            jax.ShapeDtypeStruct(far.shape, bf16),
        ],
        compiler_params=pltpu.CompilerParams(vmem_limit_bytes=60 * 2**20),
        cost_estimate=cost(HALF, FAR, 6),
        name="far_attention",
    )(chosen, queries, cot_t, near_t, lse_t, far)


def near_backward_kernel(core, queries, cot_t, keys, values, stats, att_t, far_t, *refs):
    att, att_other, q_mine, q_other, grad_k, grad_v, kv_other = refs[:7]
    grad_q, keys_t, values_t, sum_k, sum_v = refs[7:]
    keys_t[...] = keys[...].T
    values_t[...] = values[...].T
    sum_k[...] = jnp.zeros_like(sum_k)
    sum_v[...] = jnp.zeros_like(sum_v)
    columns = stats[...].T
    for piece in (0, 1):
        rows = slice(ROWS * piece, ROWS * piece + ROWS)
        width = ROWS * piece + ROWS
        for g in range(GROUP):
            cols = slice(HD * g, HD * g + HD)
            q = queries[rows, cols]
            c = cot_t[cols, rows]
            score = near_scores(q, keys_t[:, :width], piece)
            weight = jnp.exp2(score - columns[rows, g : g + 1])
            dweight = dot(c, values_t[:, :width], TN)
            dscore = (weight * (dweight - columns[rows, GROUP + g : GROUP + g + 1])).astype(bf16)
            grad = far_t[cols, rows].astype(f32).T + dot(dscore, keys[:width], NN)
            grad_q[rows, cols] = (grad * SCALE).astype(bf16)
            sum_v[:, :width] += dot(c, weight.astype(bf16), NN)
            sum_k[:, :width] += dot(q, dscore, TN)
    grad_k[...] = sum_k[...].T * SCALE
    grad_v[...] = sum_v[...].T
    for side in (0, 1):
        mine = slice(ROWS * side, ROWS * side + ROWS)
        other = slice(ROWS - ROWS * side, 2 * ROWS - ROWS * side)

        @pl.when(core[0] == side)
        def _():
            att[...] = att_t[:, mine].T
            att_other[...] = att_t[:, other].T
            q_mine[...] = grad_q[mine]
            q_other[...] = grad_q[other]
            kv_other[0] = grad_k[other].astype(bf16)
            kv_other[1] = grad_v[other].astype(bf16)


def near_backward(core, queries, cot_t, near, stats, att_t, far_t):
    wide = pl.BlockSpec((BLOCK, GROUP * HD), lambda h, c: (0, h))
    part = pl.BlockSpec((ROWS, GROUP * HD), lambda h, c: (0, h))
    tall = pl.BlockSpec((GROUP * HD, BLOCK), lambda h, c: (h, 0))
    key = pl.BlockSpec((BLOCK, HD), lambda h, c: (0, h))
    value = pl.BlockSpec((BLOCK, HD), lambda h, c: (0, HALF + h))
    rows = pl.BlockSpec((8, BLOCK), lambda h, c: (h, 0))
    both = pl.BlockSpec((2, ROWS, HD), lambda h, c: (0, 0, h))
    return pl.pallas_call(
        near_backward_kernel,
        grid_spec=pltpu.PrefetchScalarGridSpec(
            num_scalar_prefetch=1,
            grid=(HALF,),
            in_specs=[wide, tall, key, value, rows, tall, tall],
            out_specs=[part] * 4 + [key, key, both],
            scratch_shapes=[pltpu.VMEM((BLOCK, GROUP * HD), bf16)]
            + [pltpu.VMEM((HD, BLOCK), bf16)] * 2
            + [pltpu.VMEM((HD, BLOCK), f32)] * 2,
        ),
        out_shape=[jax.ShapeDtypeStruct((ROWS, queries.shape[1]), bf16)] * 4
        + [jax.ShapeDtypeStruct((BLOCK, HALF * HD), f32)] * 2
        + [jax.ShapeDtypeStruct((2, ROWS, HALF * HD), bf16)],
        compiler_params=pltpu.CompilerParams(vmem_limit_bytes=58 * 2**20),
        cost_estimate=cost(HALF, BLOCK * 3 // 4, 5),
        name="near_backward",
    )(core.reshape(1), queries, cot_t, near, near, stats, att_t, far_t)


def spread(x):
    return lax.all_to_all(x, "ctx", 0, 0, axis_index_groups=SAME_HALF, tiled=True)


def halves(x, core):
    width = x.shape[1] // 2
    mine = lax.dynamic_slice_in_dim(x, core * width, width, 1)
    return mine, lax.dynamic_slice_in_dim(x, (1 - core) * width, width, 1)


def swap(x):
    return lax.ppermute(x, "ctx", PAIR)


def in_order(mine, other, core, axis):
    return jnp.where(
        core == 0,
        jnp.concatenate([mine, other], axis=axis),
        jnp.concatenate([other, mine], axis=axis),
    )


def others_rows(x, core):
    half = x.shape[0] // 2
    return lax.dynamic_slice_in_dim(x, (1 - core) * half, half, 0)


def per_device(queries, keys, values, cotangent, selected):
    core = lax.axis_index("ctx") % 2
    my_keys, other_keys = halves(keys, core)
    my_values, other_values = halves(values, core)
    near = in_order(
        jnp.concatenate([my_keys, my_values], axis=1),
        swap(jnp.concatenate([other_keys, other_values], axis=1)),
        core,
        0,
    )
    tiles = jnp.transpose(near.reshape(BLOCKS, 8, 2 * HALF, HD), (0, 2, 1, 3))
    row = jnp.pad(selected.astype(bf16), ((0, 7), (0, HD - selected.shape[1])))
    row = jnp.broadcast_to(row[None, None], (BLOCKS, 1, 8, HD))
    tiles = jnp.concatenate([tiles, row], axis=1)
    shares = spread(tiles)
    table = shares[:, -1, 0, : 2 * KVH].astype(jnp.int32)
    table = jnp.where(core == 0, table[:, :KVH], table[:, KVH:]).reshape(-1)
    chosen = jnp.where(core == 0, selected[0, :KVH], selected[0, KVH:])
    picked = pick(table, shares)
    picked, queries, cotangent = lax.optimization_barrier((picked, queries, cotangent))
    far = spread(picked)
    got_q = swap(halves(queries, core)[1])
    got_cot = swap(halves(cotangent, core)[1])
    near_t, lse_t, block_q, cot_t = near_forward(core, queries, got_q, cotangent, got_cot, near)
    far, near_t, lse_t, cot_t = lax.optimization_barrier((far, near_t, lse_t, cot_t))
    att_t, far_t, stats, grad_far = far_attention(
        chosen, block_q, cot_t, near_t, lse_t, far
    )
    back = spread(grad_far)
    attended, other_attended, grad_q, other_q, grad_k, grad_v, near_other = near_backward(
        core, block_q, cot_t, near, stats, att_t, far_t
    )
    back, attended, grad_q, grad_k, grad_v, other_attended, other_q, near_other = (
        lax.optimization_barrier(
            (back, attended, grad_q, grad_k, grad_v, swap(other_attended), swap(other_q), swap(near_other))
        )
    )
    summed = spread(add_terms(table, back))
    attended = in_order(attended, other_attended, core, 1)
    grad_q = in_order(grad_q, other_q, core, 1)
    summed, attended, grad_q = lax.optimization_barrier((summed, attended, grad_q))
    other = swap(others_rows(summed, core))
    grad_k, grad_v = finish(core, summed, other, grad_k, grad_v, near_other)
    return attended, grad_q, grad_k, grad_v


def solution(mesh):
    specs = (P("ctx", None),) * 5
    return jax.shard_map(
        per_device, mesh=mesh, in_specs=specs, out_specs=specs[:4], check_vma=False
    )
```

```python
import math

import jax
import jax.numpy as jnp
from jax import lax
from jax.experimental import pallas as pl
from jax.experimental.pallas import tpu as pltpu
from jax.sharding import PartitionSpec as P

HD = 128
QH = 32
KVH = 8
BLOCK = 512
ROWS = 256
BLOCKS = 64
HALF = KVH // 2
GROUP = QH // KVH
FAR = 2 * BLOCK
SCALE = HD ** -0.5
SCALE_LOG2 = SCALE * math.log2(math.e)
NN = (((1,), (0,)), ((), ()))
NT = (((1,), (1,)), ((), ()))
TN = (((0,), (0,)), ((), ()))
f32 = jnp.float32
bf16 = jnp.bfloat16
LIMIT = 2.0**40

PAIR = [(i, i ^ 1) for i in range(2 * BLOCKS)]
SAME_HALF = [list(range(k, 2 * BLOCKS, 2)) for k in (0, 1)]


def pick_kernel(table, shares, out):
    step = pl.program_id(0)
    count, heads = out.shape[:2]

    def one(i, carry):
        row = (step * count + i) * 2 * heads
        for h in range(heads):
            first = jnp.maximum(table[row + 2 * h], 0)
            second = jnp.maximum(table[row + 2 * h + 1], 0)
            for kv in range(2):
                tile = kv * HALF + h
                out[i, h, kv] = jnp.concatenate([shares[first, tile], shares[second, tile]], axis=0)
        return carry

    lax.fori_loop(0, count, one, 0, unroll=8)


def pick(table, shares):
    count = 32
    return pl.pallas_call(
        pick_kernel,
        grid_spec=pltpu.PrefetchScalarGridSpec(
            num_scalar_prefetch=1,
            grid=(BLOCKS // count,),
            in_specs=[pl.BlockSpec(shares.shape, lambda i, t: (0, 0, 0, 0))],
            out_specs=pl.BlockSpec((count, HALF, 2, 16, HD), lambda i, t: (i, 0, 0, 0, 0)),
        ),
        out_shape=jax.ShapeDtypeStruct((BLOCKS, HALF, 2, 16, HD), bf16),
        compiler_params=pltpu.CompilerParams(vmem_limit_bytes=16 * 2**20),
        name="pick",
    )(table, shares)


def add_kernel(table, terms, out, total):
    step = pl.program_id(0)
    count, heads = terms.shape[:2]

    @pl.when(step == 0)
    def _():
        total[...] = jnp.zeros_like(total)

    def one(i, carry):
        row = (step * count + i) * 2 * heads
        places = []
        sums = []
        for h in range(heads):
            for e in range(2):
                block = table[row + 2 * h + e]
                slot = jnp.where(block < 0, BLOCKS, block)
                for kv in range(2):
                    place = (slot, kv * heads + h)
                    term = terms[i, h, kv].astype(f32)[8 * e : 8 * e + 8]
                    places.append(place)
                    sums.append(total[place] + term)
        for place, value in zip(places, sums):
            total[place] = value
        return carry

    lax.fori_loop(0, count, one, 0, unroll=8)

    @pl.when(step == pl.num_programs(0) - 1)
    def _():
        out[...] = total[:BLOCKS].astype(bf16)


def add_terms(table, terms):
    count = 64
    tiles = 2 * terms.shape[1]
    whole = lambda i, t: (0, 0, 0, 0)
    return pl.pallas_call(
        add_kernel,
        grid_spec=pltpu.PrefetchScalarGridSpec(
            num_scalar_prefetch=1,
            grid=(BLOCKS // count,),
            in_specs=[pl.BlockSpec((count,) + terms.shape[1:], lambda i, t: (i, 0, 0, 0, 0))],
            out_specs=pl.BlockSpec((BLOCKS, tiles, 8, HD), whole),
            scratch_shapes=[pltpu.VMEM((BLOCKS + 1, tiles, 8, HD), f32)],
        ),
        out_shape=jax.ShapeDtypeStruct((BLOCKS, tiles, 8, HD), bf16),
        compiler_params=pltpu.CompilerParams(vmem_limit_bytes=16 * 2**20),
        name="add_terms",
    )(table, terms)


def finish_kernel(core, mine, other, near_k, near_v, near_other, grad_k, grad_v):
    rows = grad_k.shape[0]
    for side, far in ((core[0], mine), (1 - core[0], other)):
        for kv, (out, near) in enumerate(((grad_k, near_k), (grad_v, near_v))):
            for h in range(HALF):
                tile = kv * HALF + h
                term = far[:, tile].astype(f32).reshape(rows, HD)
                if far is mine:
                    term += near[:, HD * h : HD * h + HD]
                else:
                    term += near_other[kv, :, HD * h : HD * h + HD].astype(f32)
                place = pl.ds(pl.multiple_of((side * HALF + h) * HD, HD), HD)
                out[:, place] = term.astype(bf16)


def finish(core, mine, other, near_k, near_v, near_other):
    steps = 2
    tiles = mine.shape[1]
    chunk = ROWS // 8 // steps
    far = pl.BlockSpec((chunk, tiles, 8, HD), lambda i, c: (i, 0, 0, 0))
    far_mine = pl.BlockSpec((chunk, tiles, 8, HD), lambda i, c: (i + steps * c[0], 0, 0, 0))
    rows = pl.BlockSpec((ROWS // steps, KVH * HD), lambda i, c: (i, 0))
    rows_mine = pl.BlockSpec((ROWS // steps, HALF * HD), lambda i, c: (i + steps * c[0], 0))
    return pl.pallas_call(
        finish_kernel,
        grid_spec=pltpu.PrefetchScalarGridSpec(
            num_scalar_prefetch=1,
            grid=(steps,),
            in_specs=[
                far_mine,
                far,
                rows_mine,
                rows_mine,
                pl.BlockSpec((2, ROWS // steps, HALF * HD), lambda i, c: (0, i, 0)),
            ],
            out_specs=[rows, rows],
        ),
        out_shape=[jax.ShapeDtypeStruct((ROWS, KVH * HD), bf16)] * 2,
        compiler_params=pltpu.CompilerParams(vmem_limit_bytes=12 * 2**20),
        name="finish",
    )(core.reshape(1), mine, other, near_k, near_v, near_other)


def dot(a, b, dims):
    return lax.dot_general(a, b, dims, preferred_element_type=f32)


def cost(heads, keys, products):
    pairs = heads * GROUP * BLOCK * keys
    return pl.CostEstimate(
        flops=products * 4 * pairs * HD, transcendentals=pairs, bytes_accessed=heads * 5 * 2**20
    )


def lanes(values):
    each = HD // len(values)
    lane = lax.broadcasted_iota(jnp.int32, (ROWS, HD), 1)
    out = jnp.broadcast_to(values[-1], (ROWS, HD))
    for i in range(len(values) - 2, -1, -1):
        out = jnp.where(lane < (i + 1) * each, values[i], out)
    return out


def near_scores(q, keys_t, piece):
    score = dot(q, keys_t, NN) * SCALE_LOG2
    shape = (ROWS, ROWS)
    causal = lax.broadcasted_iota(jnp.int32, shape, 0) >= lax.broadcasted_iota(jnp.int32, shape, 1)
    diagonal = jnp.where(causal, score[:, ROWS * piece :], -1e30)
    return jnp.concatenate([score[:, :ROWS], diagonal], axis=1) if piece else diagonal


def near_forward_kernel(
    core, my_q, got_q, my_cot, got_cot, keys, values, out_t, lse_t, queries, cot_t, cot, keys_t
):
    for side in (0, 1):
        mine = slice(ROWS * side, ROWS * side + ROWS)
        other = slice(ROWS - ROWS * side, 2 * ROWS - ROWS * side)

        @pl.when(core[0] == side)
        def _():
            queries[mine] = my_q[...]
            queries[other] = got_q[...]
            cot[mine] = my_cot[...]
            cot[other] = got_cot[...]

    keys_t[...] = keys[...].T
    cot_t[...] = cot[...].T
    for piece in (0, 1):
        rows = slice(ROWS * piece, ROWS * piece + ROWS)
        width = ROWS * piece + ROWS
        found = []
        for g in range(GROUP):
            cols = slice(HD * g, HD * g + HD)
            score = near_scores(queries[rows, cols], keys_t[:, :width], piece)
            top = jnp.max(score, axis=1, keepdims=True)
            raised = jnp.exp2(score - top)
            total = jnp.sum(raised, axis=1, keepdims=True)
            out = dot(raised.astype(bf16), values[:width], NN) * (1.0 / total)
            out_t[cols, rows] = out.T.astype(out_t.dtype)
            found.append(top + jnp.log2(total))
        lse = lanes(found).T
        for g in range(GROUP):
            lse_t[g : g + 1, rows] = lse[HD // GROUP * g : HD // GROUP * g + 1]


def near_forward(core, my_q, got_q, my_cot, got_cot, near):
    mine = pl.BlockSpec((ROWS, GROUP * HD), lambda h, c: (0, HALF * c[0] + h))
    got = pl.BlockSpec((ROWS, GROUP * HD), lambda h, c: (0, h))
    wide = pl.BlockSpec((BLOCK, GROUP * HD), lambda h, c: (0, h))
    key = pl.BlockSpec((BLOCK, HD), lambda h, c: (0, h))
    value = pl.BlockSpec((BLOCK, HD), lambda h, c: (0, HALF + h))
    tall = pl.BlockSpec((GROUP * HD, BLOCK), lambda h, c: (h, 0))
    width = HALF * GROUP * HD
    return pl.pallas_call(
        near_forward_kernel,
        grid_spec=pltpu.PrefetchScalarGridSpec(
            num_scalar_prefetch=1,
            grid=(HALF,),
            in_specs=[mine, got, mine, got, key, value],
            out_specs=[tall, pl.BlockSpec((8, BLOCK), lambda h, c: (h, 0)), wide, tall],
            scratch_shapes=[pltpu.VMEM((BLOCK, GROUP * HD), bf16), pltpu.VMEM((HD, BLOCK), bf16)],
        ),
        out_shape=[
            jax.ShapeDtypeStruct((width, BLOCK), f32),
            jax.ShapeDtypeStruct((HALF * 8, BLOCK), f32),
            jax.ShapeDtypeStruct((BLOCK, width), bf16),
            jax.ShapeDtypeStruct((width, BLOCK), bf16),
        ],
        compiler_params=pltpu.CompilerParams(vmem_limit_bytes=62 * 2**20),
        cost_estimate=cost(HALF, BLOCK * 3 // 4, 2),
        name="near_forward",
    )(core.reshape(1), my_q, got_q, my_cot, got_cot, near, near)


def far_kernel(
    chosen, queries, cot_t, near_t, lse_t, far, att_t, grad_t, stats, grad_far, keys_t, values_t, sum_k, sum_v
):
    h = pl.program_id(0)
    first = chosen[2 * h]
    second = chosen[2 * h + 1]
    keys_t[...] = far[:, 0, 0].reshape(FAR, HD).T
    values_t[...] = far[:, 0, 1].reshape(FAR, HD).T

    def one(g, masked, general):
        k = far[:, 0, 0].reshape(FAR, HD)
        v = far[:, 0, 1].reshape(FAR, HD)
        cols = pl.ds(g * HD if isinstance(g, int) else pl.multiple_of(g * HD, HD), HD)
        q = queries[:, cols]
        l0 = lse_t[pl.ds(g, 1), :]
        score = dot(k, q, NT) * SCALE_LOG2
        if masked:
            row = lax.broadcasted_iota(jnp.int32, score.shape, 0)
            entry = jnp.where(jnp.bitwise_and(row, 8) == 0, first, second)
            score = jnp.where(entry < 0, -1e30, score)
        top = jnp.maximum(jnp.max(score, axis=0, keepdims=True), l0) if general else l0
        raised = jnp.exp2(score - top)
        near = jnp.exp2(l0 - top) if general else 1.0
        total = jnp.sum(raised, axis=0, keepdims=True) + near
        over = 1.0 / total
        raised_b = raised.astype(bf16)
        out = (dot(values_t[...], raised_b, NN) + near * near_t[cols, :].astype(f32)) * over
        att_t[cols, :] = out.astype(bf16)
        cot_over = (cot_t[cols, :].astype(f32) * over).astype(bf16)
        delta = jnp.sum(cot_over.astype(f32) * out, axis=0, keepdims=True)
        dscore = (raised * (dot(v, cot_over, NN) - delta)).astype(bf16)
        grad_t[cols, :] = dot(keys_t[...], dscore, NN).astype(grad_t.dtype)
        sum_v[...] += dot(raised_b, cot_over, NT)
        sum_k[...] += dot(dscore, q, NN)
        stats[pl.ds(g, 1), :] = top + jnp.log2(total)
        stats[pl.ds(GROUP + g, 1), :] = delta * total
        return total

    def run(masked):
        worst = jnp.zeros((1, BLOCK), f32)
        for g in range(GROUP):
            worst = jnp.maximum(worst, one(g, masked, False))
        return jnp.max(worst)

    def clear():
        sum_k[...] = jnp.zeros_like(sum_k)
        sum_v[...] = jnp.zeros_like(sum_v)

    clear()
    alive = jnp.minimum(first, second) >= 0
    worst = lax.cond(alive, lambda: run(False), lambda: run(True))

    @pl.when(jnp.logical_not(worst <= LIMIT))
    def _():
        def again(g, carry):
            one(g, True, True)
            return carry

        clear()
        lax.fori_loop(0, GROUP, again, 0)

    grad_far[:, 0, 0] = (sum_k[...] * SCALE).astype(bf16).reshape(BLOCKS, 16, HD)
    grad_far[:, 0, 1] = sum_v[...].astype(bf16).reshape(BLOCKS, 16, HD)


def far_attention(chosen, queries, cot_t, near_t, lse_t, far):
    wide = pl.BlockSpec((BLOCK, GROUP * HD), lambda h, c: (0, h))
    tall = pl.BlockSpec((GROUP * HD, BLOCK), lambda h, c: (h, 0))
    rows = pl.BlockSpec((8, BLOCK), lambda h, c: (h, 0))
    gated = pl.BlockSpec((BLOCKS, 1, 2, 16, HD), lambda h, c: (0, h, 0, 0, 0))
    return pl.pallas_call(
        far_kernel,
        grid_spec=pltpu.PrefetchScalarGridSpec(
            num_scalar_prefetch=1,
            grid=(HALF,),
            in_specs=[wide, tall, tall, rows, gated],
            out_specs=[tall, tall, rows, gated],
            scratch_shapes=[pltpu.VMEM((HD, FAR), bf16)] * 2 + [pltpu.VMEM((FAR, HD), f32)] * 2,
        ),
        out_shape=[
            jax.ShapeDtypeStruct(cot_t.shape, bf16),
            jax.ShapeDtypeStruct(cot_t.shape, f32),
            jax.ShapeDtypeStruct(lse_t.shape, f32),
            jax.ShapeDtypeStruct(far.shape, bf16),
        ],
        compiler_params=pltpu.CompilerParams(vmem_limit_bytes=60 * 2**20),
        cost_estimate=cost(HALF, FAR, 6),
        name="far_attention",
    )(chosen, queries, cot_t, near_t, lse_t, far)


def near_backward_kernel(core, queries, cot_t, keys, values, stats, att_t, far_t, *refs):
    att, att_other, q_mine, q_other, grad_k, grad_v, kv_other = refs[:7]
    grad_q, keys_t, values_t, sum_k, sum_v = refs[7:]
    keys_t[...] = keys[...].T
    values_t[...] = values[...].T
    sum_k[...] = jnp.zeros_like(sum_k)
    sum_v[...] = jnp.zeros_like(sum_v)
    columns = stats[...].T
    for piece in (0, 1):
        rows = slice(ROWS * piece, ROWS * piece + ROWS)
        width = ROWS * piece + ROWS
        for g in range(GROUP):
            cols = slice(HD * g, HD * g + HD)
            q = queries[rows, cols]
            c = cot_t[cols, rows]
            score = near_scores(q, keys_t[:, :width], piece)
            weight = jnp.exp2(score - columns[rows, g : g + 1])
            dweight = dot(c, values_t[:, :width], TN)
            dscore = (weight * (dweight - columns[rows, GROUP + g : GROUP + g + 1])).astype(bf16)
            grad = far_t[cols, rows].astype(f32).T + dot(dscore, keys[:width], NN)
            grad_q[rows, cols] = (grad * SCALE).astype(bf16)
            sum_v[:, :width] += dot(c, weight.astype(bf16), NN)
            sum_k[:, :width] += dot(q, dscore, TN)
    grad_k[...] = sum_k[...].T * SCALE
    grad_v[...] = sum_v[...].T
    for side in (0, 1):
        mine = slice(ROWS * side, ROWS * side + ROWS)
        other = slice(ROWS - ROWS * side, 2 * ROWS - ROWS * side)

        @pl.when(core[0] == side)
        def _():
            att[...] = att_t[:, mine].T
            att_other[...] = att_t[:, other].T
            q_mine[...] = grad_q[mine]
            q_other[...] = grad_q[other]
            kv_other[0] = grad_k[other].astype(bf16)
            kv_other[1] = grad_v[other].astype(bf16)


def near_backward(core, queries, cot_t, near, stats, att_t, far_t):
    wide = pl.BlockSpec((BLOCK, GROUP * HD), lambda h, c: (0, h))
    part = pl.BlockSpec((ROWS, GROUP * HD), lambda h, c: (0, h))
    tall = pl.BlockSpec((GROUP * HD, BLOCK), lambda h, c: (h, 0))
    key = pl.BlockSpec((BLOCK, HD), lambda h, c: (0, h))
    value = pl.BlockSpec((BLOCK, HD), lambda h, c: (0, HALF + h))
    rows = pl.BlockSpec((8, BLOCK), lambda h, c: (h, 0))
    both = pl.BlockSpec((2, ROWS, HD), lambda h, c: (0, 0, h))
    return pl.pallas_call(
        near_backward_kernel,
        grid_spec=pltpu.PrefetchScalarGridSpec(
            num_scalar_prefetch=1,
            grid=(HALF,),
            in_specs=[wide, tall, key, value, rows, tall, tall],
            out_specs=[part] * 4 + [key, key, both],
            scratch_shapes=[pltpu.VMEM((BLOCK, GROUP * HD), bf16)]
            + [pltpu.VMEM((HD, BLOCK), bf16)] * 2
            + [pltpu.VMEM((HD, BLOCK), f32)] * 2,
        ),
        out_shape=[jax.ShapeDtypeStruct((ROWS, queries.shape[1]), bf16)] * 4
        + [jax.ShapeDtypeStruct((BLOCK, HALF * HD), f32)] * 2
        + [jax.ShapeDtypeStruct((2, ROWS, HALF * HD), bf16)],
        compiler_params=pltpu.CompilerParams(vmem_limit_bytes=58 * 2**20),
        cost_estimate=cost(HALF, BLOCK * 3 // 4, 5),
        name="near_backward",
    )(core.reshape(1), queries, cot_t, near, near, stats, att_t, far_t)


def spread(x):
    return lax.all_to_all(x, "ctx", 0, 0, axis_index_groups=SAME_HALF, tiled=True)


def halves(x, core):
    width = x.shape[1] // 2
    mine = lax.dynamic_slice_in_dim(x, core * width, width, 1)
    return mine, lax.dynamic_slice_in_dim(x, (1 - core) * width, width, 1)


def swap(x):
    return lax.ppermute(x, "ctx", PAIR)


def in_order(mine, other, core, axis):
    return jnp.where(
        core == 0,
        jnp.concatenate([mine, other], axis=axis),
        jnp.concatenate([other, mine], axis=axis),
    )


def others_rows(x, core):
    half = x.shape[0] // 2
    return lax.dynamic_slice_in_dim(x, (1 - core) * half, half, 0)


def per_device(queries, keys, values, cotangent, selected):
    core = lax.axis_index("ctx") % 2
    my_keys, other_keys = halves(keys, core)
    my_values, other_values = halves(values, core)
    near = in_order(
        jnp.concatenate([my_keys, my_values], axis=1),
        swap(jnp.concatenate([other_keys, other_values], axis=1)),
        core,
        0,
    )
    tiles = jnp.transpose(near.reshape(BLOCKS, 8, 2 * HALF, HD), (0, 2, 1, 3))
    row = jnp.pad(selected.astype(bf16), ((0, 7), (0, HD - selected.shape[1])))
    row = jnp.broadcast_to(row[None, None], (BLOCKS, 1, 8, HD))
    tiles = jnp.concatenate([tiles, row], axis=1)
    shares = spread(tiles)
    table = shares[:, -1, 0, : 2 * KVH].astype(jnp.int32)
    table = jnp.where(core == 0, table[:, :KVH], table[:, KVH:]).reshape(-1)
    chosen = jnp.where(core == 0, selected[0, :KVH], selected[0, KVH:])
    picked = pick(table, shares)
    picked, queries, cotangent = lax.optimization_barrier((picked, queries, cotangent))
    far = spread(picked)
    got_q = swap(halves(queries, core)[1])
    got_cot = swap(halves(cotangent, core)[1])
    near_t, lse_t, block_q, cot_t = near_forward(core, queries, got_q, cotangent, got_cot, near)
    far, near_t, lse_t, cot_t = lax.optimization_barrier((far, near_t, lse_t, cot_t))
    att_t, far_t, stats, grad_far = far_attention(
        chosen, block_q, cot_t, near_t, lse_t, far
    )
    back = spread(grad_far)
    attended, other_attended, grad_q, other_q, grad_k, grad_v, near_other = near_backward(
        core, block_q, cot_t, near, stats, att_t, far_t
    )
    back, attended, grad_q, grad_k, grad_v, other_attended, other_q, near_other = (
        lax.optimization_barrier(
            (back, attended, grad_q, grad_k, grad_v, swap(other_attended), swap(other_q), swap(near_other))
        )
    )
    summed = spread(add_terms(table, back))
    attended = in_order(attended, other_attended, core, 1)
    grad_q = in_order(grad_q, other_q, core, 1)
    summed, attended, grad_q = lax.optimization_barrier((summed, attended, grad_q))
    other = swap(others_rows(summed, core))
    grad_k, grad_v = finish(core, summed, other, grad_k, grad_v, near_other)
    return attended, grad_q, grad_k, grad_v


def solution(mesh):
    specs = (P("ctx", None),) * 5
    return jax.shard_map(
        per_device, mesh=mesh, in_specs=specs, out_specs=specs[:4], check_vma=False
    )
```
